32 devices in a mesh: pole: 2 (over x), prow: 8 (over z, y), pcol: 2 (over core).
Axes of the slice: x: 2, y: 2, z: 4, core: 2. Of those that a mesh axis runs over, the one named last changes fastest.
Arguments:
- ancestor_inverse: bfloat16 [8192, 4096], P(('pole', 'prow'), 'pcol'), parts along dimension 0, may hold values from -6 to 6
- l_panel: bfloat16 [8192, 1024], P(('pole', 'prow'), 'pcol'), parts along dimension 0, may hold values from -0.125 to 0.125
- diag_inverse: float32 [2048, 256], P(('pole', 'pcol')), parts along dimension 0, may hold values from -6 to 6
- pattern: int32 [4, 8], replicated, may hold values from 0 to 15, as said below
Outputs:
- column_blocks: float32 [8192, 1024], P(('pole', 'prow'), 'pcol'), parts along dimension 0
- diag_blocks: float32 [2048, 256], P(('pole', 'pcol')), parts along dimension 0
The draws below stay inside these ranges and needn't reach their ends.
There are 2 independent parts, one for each index of `pole`. The reference program is written for one: setup_inputs(seed, part) draws one part's arguments, and reference() takes and returns one part's arrays. A program takes and returns all parts, laid end to end along the dimension named above; an argument that names none is the same for every part. Nothing has to cross between parts.
Inputs may be any that keep to these rules, and one draw needn't show every extreme that they name: `pattern`: each row lists 8 different ancestor supernodes in increasing order, and every row lists ancestor 16 - 1.
All inputs are finite; a program needn't handle non-finite values.
Results may differ from the reference program's by a relative error of at most 0.0003.
Values may be sent and summed in bfloat16 or wider, within the bound.
A program may use at most 128 MiB of HBM per device.

```python
import jax
import jax.numpy as jnp
import numpy as np
from jax import lax

B = 256
RT = 2
NK = 4
NA = 16
S = 8
N_PCOL = 2


def draw_pattern(key, part):
    scores = jax.random.randint(key, (NK, NA), 0, 2 * NA)
    positions = jnp.arange(NA, dtype=jnp.int32)
    scores = (scores + positions[None, :]) * NA + positions[None, :]
    scores = scores.at[:, NA - 1].set(4 * NA * NA)
    _, chosen = lax.top_k(scores, S)
    return jnp.sort(chosen, axis=1).astype(jnp.int32)


def levels(rng, dims, cuts, least, high):
    level = 1.0
    for axis_at, shards_of in cuts:
        steps = jax.random.uniform(jax.random.fold_in(jax.random.fold_in(rng, 6), axis_at), (shards_of,), jnp.float32, least / len(cuts), high / len(cuts))
        level = level * jnp.repeat(jnp.exp(steps), dims[axis_at] // shards_of).reshape((-1,) + (1,) * (len(dims) - 1 - axis_at))
    return level


def bell_draw(own_key, dims, deviation, reach, cuts=(), kind=jnp.bfloat16):
    result = jax.random.normal(own_key, dims, jnp.float32) * deviation
    if len(cuts) > 0:
        result = levels(own_key, dims, cuts, -0.22, 0.18) * result
    return jnp.clip(result, min=-reach, max=reach).astype(kind)


def setup_inputs(seed: int = 0, part: int = 0) -> dict:
    keys = jax.random.split(jax.random.key(seed), 5)
    own_keys = jax.random.split(jax.random.fold_in(keys[4], part), 5)
    ancestor_inverse = bell_draw(own_keys[0], (NA * B, NA * B), 1.0, 6.0, ((0, 8), (1, 2)))
    l_panel = bell_draw(own_keys[1], (NA * B, NK * B), (S * B) ** -0.5, 0.125, ((0, 8), (1, 2)))
    diag_inverse = bell_draw(own_keys[2], (NK * B, B), 1.0, 6.0, ((0, 2),), jnp.float32)
    pattern = draw_pattern(jax.random.fold_in(keys[4], 71), part)
    return {"ancestor_inverse": ancestor_inverse, "l_panel": l_panel, "diag_inverse": diag_inverse, "pattern": pattern}


def reference(ancestor_inverse, l_panel, diag_inverse, pattern):
    share = RT // N_PCOL
    per_column = NA // N_PCOL
    stored = np.arange(NA)
    column_part = stored // per_column
    remain = stored % per_column
    tile_order = (remain // share) * RT + column_part * share + remain % share
    tile_ids = jnp.arange(NA, dtype=jnp.int32)
    member = jnp.any(pattern[None, :, :] == tile_ids[:, None, None], axis=2).astype(jnp.float32)
    panel_mask = member[:, None, :, None]
    masked = (l_panel.reshape(NA, B, NK, B) * panel_mask.astype(jnp.bfloat16)).reshape(NA * B, NK * B)
    ordered = masked.reshape(NA, B, NK * B)[tile_order].reshape(NA * B, NK * B)
    product_full = -jnp.dot(ancestor_inverse, ordered, preferred_element_type=jnp.float32)
    column_blocks = (product_full.reshape(NA, B, NK, B) * panel_mask).reshape(NA * B, NK * B).astype(jnp.float32)
    diag_terms = jnp.einsum("rkb,rkc->kbc", masked.astype(jnp.float32).reshape(NA * B, NK, B),
                            product_full.reshape(NA * B, NK, B), precision=lax.Precision.HIGHEST)
    diag_blocks = diag_inverse - diag_terms.reshape(NK * B, B)
    return column_blocks, diag_blocks
```

```python
import functools

import jax
import jax.numpy as jnp
from jax import lax
from jax.experimental import pallas as pl
from jax.experimental.pallas import tpu as pltpu
from jax.sharding import PartitionSpec as P

MESH = pl.DeviceIdType.MESH
NY = 2
N_COL = 2
NH = 2
SKEW = 2


def kernel(cfg, a_hbm, l_ref, d_ref, pat, out_ref, diag_ref, a_full, own, ubuf, dbuf, sd, su, fin, yin, acc,
           part, yr, ysum, zr, tot, ytot, a_sem, ph_ss, ph_rs, sd_ss, u_rs, su_ss, d_rs, fin_ss, y_rs, r_sem, zs_ss, zs_rs,
           zg_ss, zg_rs):
    nz, rt, share, na, s_n, b = cfg
    bh = b // NH
    tz = rt * NY
    row = lax.axis_index("prow")
    c = lax.axis_index("pcol")
    y = lax.rem(row, NY)
    z = row // NY
    oy = NY - 1 - y
    ypeer = {"prow": z * NY + oy}
    cpeer = {"pcol": 1 - c}

    def zdev(zz):
        return {"prow": zz * NY + y}

    barrier = pltpu.get_barrier_semaphore()
    pl.semaphore_signal(barrier, inc=1, device_id=ypeer, device_id_type=MESH)
    pl.semaphore_signal(barrier, inc=1, device_id=cpeer, device_id_type=MESH)
    for d in range(1, nz):
        pl.semaphore_signal(barrier, inc=1, device_id=zdev(lax.rem(z + d, nz)), device_id_type=MESH)
    acc[...] = jnp.zeros_like(acc)
    n_a = na // N_COL

    def a_local(i):
        return pltpu.make_async_copy(a_hbm.at[:, i * b:(i + 1) * b], a_full.at[c, i], a_sem.at[0, i])

    for i in range(n_a):
        a_local(i).start()
    pl.semaphore_wait(barrier, nz + 1)

    def remote(src, dst, ss, rs, dev):
        return pltpu.make_async_remote_copy(src_ref=src, dst_ref=dst, send_sem=ss, recv_sem=rs, device_id=dev,
                                            device_id_type=MESH)

    def a_send(i):
        return remote(a_hbm.at[:, i * b:(i + 1) * b], a_full.at[c, i], a_sem.at[1, i], a_sem.at[2, i], cpeer)

    def phase1(h, i):
        lanes = pl.ds(pl.multiple_of(oy * b + h * bh, 128), bh)
        return remote(l_ref.at[i * b:(i + 1) * b, lanes], own.at[h, y * rt + i], ph_ss.at[h, i], ph_rs.at[h, i], ypeer)

    for h in range(NH):
        for i in range(rt):
            phase1(h, i).start()
    for i in range(n_a):
        a_send(i).start()
    for h in range(NH):
        lanes = pl.ds(pl.multiple_of(y * b + h * bh, 128), bh)
        for i in range(rt):
            own[h, y * rt + i] = l_ref[i * b:(i + 1) * b, lanes]
    for i in range(rt):
        phase1(0, i).wait_recv()

    below = lax.rem(z + nz - 1, nz)
    above = lax.rem(z + 1, nz)

    def down(h, j):
        return remote(sd.at[h, j], ubuf.at[h, j], sd_ss.at[h, j], u_rs.at[h, j], zdev(below))

    def up(h, j):
        return remote(su.at[h, j], dbuf.at[h, j], su_ss.at[h, j], d_rs.at[h, j], zdev(above))

    def across(h, j):
        return remote(fin.at[h, j], yin.at[h, j], fin_ss.at[h, j], y_rs.at[h, j], ypeer)

    nodes = l_ref.shape[1] // b
    zc = min((na - s_n) // tz, nz - 1)
    j0 = jnp.maximum(tz * z - (na - s_n), 0)
    lag_d = SKEW * jnp.maximum(zc - z, 0)
    lag_u = SKEW * z
    lag_f = jnp.maximum(lag_d, lag_u)
    total = NH * s_n

    def tile_of(k, j):
        return pat[c * nodes + k, j]

    def own_tile(h, t):
        v = own[h, 0]
        for i in range(1, tz):
            v = lax.select(t == tz * z + i, own[h, i], v)
        return v

    def a_tile(t):
        part_at = lax.rem(t, rt) // share
        li = (t // rt) * share + lax.rem(t, share)
        return a_full[part_at, li]

    def step(s, carry):
        @pl.when(s == s_n)
        def _():
            for h in range(1, NH):
                for i in range(rt):
                    phase1(h, i).wait_recv()

        @pl.when(s == SKEW)
        def _():
            for i in range(n_a):
                a_local(i).wait()
                a_send(i).wait()

        pd = s - lag_d
        hd, jd = pd // s_n, j0 + lax.rem(pd, s_n)
        live = (pd >= 0) & (pd < total) & (jd < s_n)

        @pl.when(live & (z < nz - 1) & (jd + (na - s_n) >= tz * (z + 1)))
        def _():
            down(hd, jd).wait_recv()

        @pl.when(live & (z > 0))
        def _():
            t = tile_of(y, jd)
            sd[hd, jd] = lax.select(t < tz * (z + 1), own_tile(hd, t), ubuf[hd, jd])
            down(hd, jd).start()

        pu = s - lag_u
        hu, ju = pu // s_n, lax.rem(pu, s_n)
        live_u = (pu >= 0) & (pu < total) & (ju < s_n - 1)

        @pl.when(live_u & (z > 0) & (ju < tz * z))
        def _():
            up(hu, ju).wait_recv()

        @pl.when(live_u & (z < nz - 1) & (ju < tz * (z + 1)))
        def _():
            t = tile_of(y, ju)
            su[hu, ju] = lax.select(t >= tz * z, own_tile(hu, t), dbuf[hu, ju])
            up(hu, ju).start()

        pf = s - lag_f
        hf, jf = pf // s_n, lax.rem(pf, s_n)

        @pl.when((pf >= 0) & (pf < total))
        def _():
            t = tile_of(y, jf)
            v = lax.select(t < tz * z, dbuf[hf, jf], own_tile(hf, t))
            v = lax.select(t >= tz * (z + 1), ubuf[hf, jf], v)
            fin[hf, jf] = v
            across(hf, jf).start()
            acc[y, hf] += jnp.dot(a_tile(t), v, preferred_element_type=jnp.float32)

        py = pf - SKEW
        hy, jy = py // s_n, lax.rem(py, s_n)

        @pl.when((py >= 0) & (py < total))
        def _():
            across(hy, jy).wait_recv()
            t = tile_of(oy, jy)
            acc[oy, hy] += jnp.dot(a_tile(t), yin[hy, jy], preferred_element_type=jnp.float32)

        return carry

    lax.fori_loop(0, total + SKEW * nz, step, 0)

    for k in range(nodes):
        for i in range(rt):
            t = row * rt + i
            hit = pat[c * nodes + k, 0] == t
            for j in range(1, s_n):
                hit = hit | (pat[c * nodes + k, j] == t)
            m = -jnp.where(hit, 1.0, 0.0).astype(jnp.float32)
            for h in range(NH):
                out_ref[i * b:(i + 1) * b, k * b + h * bh:k * b + (h + 1) * bh] = acc[k, h, i * b:(i + 1) * b, :] * m
        x = out_ref[:, k * b:(k + 1) * b]
        hi = x.astype(jnp.bfloat16)
        lo = (x - hi.astype(jnp.float32)).astype(jnp.bfloat16)
        lk = l_ref[:, k * b:(k + 1) * b]
        dims = (((0,), (0,)), ((), ()))
        part[k] = lax.dot_general(lk, hi, dims, preferred_element_type=jnp.float32) + lax.dot_general(
            lk, lo, dims, preferred_element_type=jnp.float32)

    first = remote(part.at[oy], yr, r_sem.at[0], r_sem.at[1], ypeer)
    first.start()
    first.wait()
    ysum[...] = part[y] + yr[...]
    ch = b // nz

    def rs(d, src):
        to = lax.rem(z + d, nz)
        return remote(ysum.at[pl.ds(pl.multiple_of(to * ch, 8), ch), :], zr.at[d], zs_ss.at[d], zs_rs.at[d], zdev(to))

    for d in range(1, nz):
        rs(d, z).start()
    mine = pl.ds(pl.multiple_of(z * ch, 8), ch)
    total_z = ysum[mine, :]
    for d in range(1, nz):
        rs(d, z).wait_recv()
        total_z = total_z + zr[d]
    tot[mine, :] = total_z

    def ag(d):
        to = lax.rem(z + d, nz)
        return remote(tot.at[mine, :], tot.at[mine, :], zg_ss.at[d], zg_rs.at[d], zdev(to))

    def ag_in(d):
        at = lax.rem(z + nz - d, nz)
        there = pl.ds(pl.multiple_of(at * ch, 8), ch)
        return remote(tot.at[there, :], tot.at[there, :], zg_ss.at[d], zg_rs.at[d], zdev(at))

    for d in range(1, nz):
        ag(d).start()
    for d in range(1, nz):
        ag_in(d).wait_recv()
    last = remote(tot, ytot, r_sem.at[2], r_sem.at[3], ypeer)
    last.start()
    at_y = pl.ds(pl.multiple_of(y * b, 8), b)
    at_o = pl.ds(pl.multiple_of(oy * b, 8), b)
    diag_ref[at_y, :] = d_ref[at_y, :] - tot[...]

    for h in range(NH):
        for i in range(rt):
            phase1(h, i).wait_send()

    def drain(p, carry):
        h, j = p // s_n, lax.rem(p, s_n)

        @pl.when((z > 0) & (j >= j0))
        def _():
            down(h, j).wait_send()

        @pl.when((z < nz - 1) & (j < s_n - 1) & (j < tz * (z + 1)))
        def _():
            up(h, j).wait_send()

        across(h, j).wait_send()
        return carry

    lax.fori_loop(0, total, drain, 0)
    for d in range(1, nz):
        rs(d, z).wait_send()
        ag(d).wait_send()
    last.wait()
    diag_ref[at_o, :] = d_ref[at_o, :] - ytot[...]


def solution(mesh):
    n_row, n_col = mesh.shape["prow"], mesh.shape["pcol"]
    nz = n_row // NY

    def per_device(ancestor_inverse, l_panel, diag_inverse, pattern):
        b = diag_inverse.shape[1]
        rt = l_panel.shape[0] // b
        nodes = l_panel.shape[1] // b
        na, s_n = rt * n_row, pattern.shape[1]
        share = rt // n_col
        bh = b // NH
        bf, f32 = jnp.bfloat16, jnp.float32
        slots = pltpu.VMEM((NH, s_n, b, bh), bf)
        sems = pltpu.SemaphoreType.DMA((NH, s_n))
        zsem = pltpu.SemaphoreType.DMA((nz,))
        vmem = pl.BlockSpec(memory_space=pltpu.VMEM)
        return pl.pallas_call(
            functools.partial(kernel, (nz, rt, share, na, s_n, b)),
            out_shape=(jax.ShapeDtypeStruct(l_panel.shape, f32), jax.ShapeDtypeStruct(diag_inverse.shape, f32)),
            in_specs=[pl.BlockSpec(memory_space=pl.ANY), vmem, vmem, pl.BlockSpec(memory_space=pltpu.SMEM)],
            out_specs=(vmem, vmem),
            scratch_shapes=[
                pltpu.VMEM((n_col, na // n_col, rt * b, b), bf),
                pltpu.VMEM((NH, rt * NY, b, bh), bf),
                slots, slots, slots, slots, slots, slots,
                pltpu.VMEM((nodes, NH, rt * b, bh), f32),
                pltpu.VMEM((nodes, b, b), f32),
                pltpu.VMEM((b, b), f32),
                pltpu.VMEM((b, b), f32),
                pltpu.VMEM((nz, b // nz, b), f32),
                pltpu.VMEM((b, b), f32),
                pltpu.VMEM((b, b), f32),
                pltpu.SemaphoreType.DMA((3, na // n_col)),
                pltpu.SemaphoreType.DMA((NH, rt)),
                pltpu.SemaphoreType.DMA((NH, rt)),
                sems, sems, sems, sems, sems, sems,
                pltpu.SemaphoreType.DMA((4,)),
                zsem, zsem, zsem, zsem,
            ],
            compiler_params=pltpu.CompilerParams(collective_id=0, has_side_effects=True, vmem_limit_bytes=56 * 2**20),
            cost_estimate=pl.CostEstimate(flops=4 * 10**9, bytes_accessed=2**23, transcendentals=0),
        )(ancestor_inverse, l_panel, diag_inverse, pattern)

    return jax.shard_map(
        per_device,
        mesh=mesh,
        in_specs=(P(("pole", "prow"), "pcol"), P(("pole", "prow"), "pcol"), P(("pole", "pcol"), None), P()),
        out_specs=(P(("pole", "prow"), "pcol"), P(("pole", "pcol"), None)),
        check_vma=False,
    )
```

```python
import functools

import jax
import jax.numpy as jnp
from jax import lax
from jax.experimental import pallas as pl
from jax.experimental.pallas import tpu as pltpu
from jax.sharding import PartitionSpec as P

MESH = pl.DeviceIdType.MESH
NY = 2
N_COL = 2
NH = 2
GAP = 3
SKEW = 2


def kernel(cfg, a_hbm, l_ref, d_ref, pat, out_ref, diag_ref, a_full, own, ubuf, dbuf, sd, su, fin, yin, acc,
           part, yr, ysum, zr, tot, ytot, a_sem, ph_ss, ph_rs, sd_ss, u_rs, su_ss, d_rs, fin_ss, y_rs, r_sem, zs_ss, zs_rs,
           zg_ss, zg_rs):
    nz, rt, share, na, s_n, b = cfg
    bh = b // NH
    tz = rt * NY
    row = lax.axis_index("prow")
    c = lax.axis_index("pcol")
    y = lax.rem(row, NY)
    z = row // NY
    oy = NY - 1 - y
    ypeer = {"prow": z * NY + oy}
    cpeer = {"pcol": 1 - c}

    def zdev(zz):
        return {"prow": zz * NY + y}

    barrier = pltpu.get_barrier_semaphore()
    pl.semaphore_signal(barrier, inc=1, device_id=ypeer, device_id_type=MESH)
    pl.semaphore_signal(barrier, inc=1, device_id=cpeer, device_id_type=MESH)
    for d in range(1, nz):
        pl.semaphore_signal(barrier, inc=1, device_id=zdev(lax.rem(z + d, nz)), device_id_type=MESH)
    acc[...] = jnp.zeros_like(acc)
    n_a = na // N_COL

    def a_local(i):
        return pltpu.make_async_copy(a_hbm.at[:, i * b:(i + 1) * b], a_full.at[c, i], a_sem.at[0, i])

    for i in range(n_a):
        a_local(i).start()
    pl.semaphore_wait(barrier, nz + 1)

    def remote(src, dst, ss, rs, dev):
        return pltpu.make_async_remote_copy(src_ref=src, dst_ref=dst, send_sem=ss, recv_sem=rs, device_id=dev,
                                            device_id_type=MESH)

    def a_send(i):
        return remote(a_hbm.at[:, i * b:(i + 1) * b], a_full.at[c, i], a_sem.at[1, i], a_sem.at[2, i], cpeer)

    def phase1(h, i):
        lanes = pl.ds(pl.multiple_of(oy * b + h * bh, 128), bh)
        return remote(l_ref.at[i * b:(i + 1) * b, lanes], own.at[h, y * rt + i], ph_ss.at[h, i], ph_rs.at[h, i], ypeer)

    for h in range(NH):
        for i in range(rt):
            phase1(h, i).start()
    for i in range(n_a):
        a_send(i).start()
    for h in range(NH):
        lanes = pl.ds(pl.multiple_of(y * b + h * bh, 128), bh)
        for i in range(rt):
            own[h, y * rt + i] = l_ref[i * b:(i + 1) * b, lanes]
    for i in range(rt):
        phase1(0, i).wait_recv()

    below = lax.rem(z + nz - 1, nz)
    above = lax.rem(z + 1, nz)

    def down(h, j):
        return remote(sd.at[h, j], ubuf.at[h, j], sd_ss.at[h, j], u_rs.at[h, j], zdev(below))

    def up(h, j):
        return remote(su.at[h, j], dbuf.at[h, j], su_ss.at[h, j], d_rs.at[h, j], zdev(above))

    def across(h, j):
        return remote(fin.at[h, j], yin.at[h, j], fin_ss.at[h, j], y_rs.at[h, j], ypeer)

    nodes = l_ref.shape[1] // b
    zc = min((na - s_n) // tz, nz - 1)
    j0 = jnp.maximum(tz * z - (na - s_n), 0)
    lag_d = SKEW * jnp.maximum(zc - z, 0)
    lag_u = SKEW * z
    lag_f = jnp.maximum(lag_d, lag_u)
    total = NH * s_n

    def tile_of(k, j):
        return pat[c * nodes + k, j]

    def own_tile(h, t):
        v = own[h, 0]
        for i in range(1, tz):
            v = lax.select(t == tz * z + i, own[h, i], v)
        return v

    def a_tile(t):
        part_at = lax.rem(t, rt) // share
        li = (t // rt) * share + lax.rem(t, share)
        return a_full[part_at, li]

    ch = b // nz
    at_y = pl.ds(pl.multiple_of(y * b, 8), b)
    at_o = pl.ds(pl.multiple_of(oy * b, 8), b)
    mine = pl.ds(pl.multiple_of(z * ch, 8), ch)

    def first(h):
        return remote(part.at[h, oy], yr.at[h], r_sem.at[h, 0], r_sem.at[h, 1], ypeer)

    def last(h):
        return remote(tot.at[h], ytot.at[h], r_sem.at[h, 2], r_sem.at[h, 3], ypeer)

    def rs(h, d):
        to = lax.rem(z + d, nz)
        return remote(ysum.at[h, pl.ds(pl.multiple_of(to * ch, 8), ch), :], zr.at[h, d], zs_ss.at[h, d],
                      zs_rs.at[h, d], zdev(to))

    def ag(h, d):
        to = lax.rem(z + d, nz)
        return remote(tot.at[h, mine, :], tot.at[h, mine, :], zg_ss.at[h, d], zg_rs.at[h, d], zdev(to))

    def ag_in(h, d):
        at = lax.rem(z + nz - d, nz)
        there = pl.ds(pl.multiple_of(at * ch, 8), ch)
        return remote(tot.at[h, there, :], tot.at[h, there, :], zg_ss.at[h, d], zg_rs.at[h, d], zdev(at))

    def reduce_0(h):
        for k in range(nodes):
            at = slice(k * b + h * bh, k * b + (h + 1) * bh)
            for i in range(rt):
                t = row * rt + i
                hit = pat[c * nodes + k, 0] == t
                for j in range(1, s_n):
                    hit = hit | (pat[c * nodes + k, j] == t)
                m = -jnp.where(hit, 1.0, 0.0).astype(jnp.float32)
                out_ref[i * b:(i + 1) * b, at] = acc[k, h, i * b:(i + 1) * b, :] * m
            x = out_ref[:, at]
            hi = x.astype(jnp.bfloat16)
            lo = (x - hi.astype(jnp.float32)).astype(jnp.bfloat16)
            both = lax.dot_general(l_ref[:, k * b:(k + 1) * b], jnp.concatenate([hi, lo], axis=1),
                                   (((0,), (0,)), ((), ())), preferred_element_type=jnp.float32)
            part[h, k] = both[:, :bh] + both[:, bh:]
        first(h).start()

    def reduce_1(h):
        first(h).wait()
        ysum[h] = part[h, y] + yr[h]
        for d in range(1, nz):
            rs(h, d).start()

    def reduce_2(h):
        total_z = ysum[h, mine, :]
        for d in range(1, nz):
            rs(h, d).wait_recv()
            total_z = total_z + zr[h, d]
        tot[h, mine, :] = total_z
        for d in range(1, nz):
            ag(h, d).start()

    def reduce_3(h):
        for d in range(1, nz):
            ag_in(h, d).wait_recv()
        last(h).start()
        lanes = slice(h * bh, (h + 1) * bh)
        diag_ref[at_y, lanes] = d_ref[at_y, lanes] - tot[h]

    def reduce_4(h):
        lanes = slice(h * bh, (h + 1) * bh)
        last(h).wait_recv()
        diag_ref[at_o, lanes] = d_ref[at_o, lanes] - ytot[h]

    def step(s, carry):
        @pl.when(s == s_n)
        def _():
            for h in range(1, NH):
                for i in range(rt):
                    phase1(h, i).wait_recv()

        @pl.when(s == SKEW)
        def _():
            for i in range(n_a):
                a_local(i).wait()
                a_send(i).wait()

        pd = s - lag_d
        hd, jd = pd // s_n, j0 + lax.rem(pd, s_n)
        live = (pd >= 0) & (pd < total) & (jd < s_n)

        @pl.when(live & (z < nz - 1) & (jd + (na - s_n) >= tz * (z + 1)))
        def _():
            down(hd, jd).wait_recv()

        @pl.when(live & (z > 0))
        def _():
            t = tile_of(y, jd)
            sd[hd, jd] = lax.select(t < tz * (z + 1), own_tile(hd, t), ubuf[hd, jd])
            down(hd, jd).start()

        pu = s - lag_u
        hu, ju = pu // s_n, lax.rem(pu, s_n)
        live_u = (pu >= 0) & (pu < total) & (ju < s_n - 1)

        @pl.when(live_u & (z > 0) & (ju < tz * z))
        def _():
            up(hu, ju).wait_recv()

        @pl.when(live_u & (z < nz - 1) & (ju < tz * (z + 1)))
        def _():
            t = tile_of(y, ju)
            su[hu, ju] = lax.select(t >= tz * z, own_tile(hu, t), dbuf[hu, ju])
            up(hu, ju).start()

        pf = s - lag_f
        hf, jf = pf // s_n, lax.rem(pf, s_n)

        @pl.when((pf >= 0) & (pf < total))
        def _():
            t = tile_of(y, jf)
            v = lax.select(t < tz * z, dbuf[hf, jf], own_tile(hf, t))
            v = lax.select(t >= tz * (z + 1), ubuf[hf, jf], v)
            fin[hf, jf] = v
            across(hf, jf).start()
            acc[y, hf] += jnp.dot(a_tile(t), v, preferred_element_type=jnp.float32)

        py = pf - SKEW
        hy, jy = py // s_n, lax.rem(py, s_n)

        @pl.when((py >= 0) & (py < total))
        def _():
            across(hy, jy).wait_recv()
            t = tile_of(oy, jy)
            acc[oy, hy] += jnp.dot(a_tile(t), yin[hy, jy], preferred_element_type=jnp.float32)

        for h in range(NH - 1):
            done = (h + 1) * s_n + SKEW

            @pl.when(s == done + lag_f)
            def _(h=h):
                reduce_0(h)

            @pl.when(s == done + lag_f + GAP)
            def _(h=h):
                reduce_1(h)

            @pl.when(s == done + SKEW * (nz - 1) + 2 * GAP)
            def _(h=h):
                reduce_2(h)

        return carry

    lax.fori_loop(0, total + SKEW * nz, step, 0)

    for h in range(NH - 1):
        reduce_3(h)
    h = NH - 1
    reduce_0(h)
    for g in range(NH - 1):
        reduce_4(g)
    reduce_1(h)
    reduce_2(h)
    reduce_3(h)

    for g in range(NH):
        for i in range(rt):
            phase1(g, i).wait_send()

    def drain(p, carry):
        g, j = p // s_n, lax.rem(p, s_n)

        @pl.when((z > 0) & (j >= j0))
        def _():
            down(g, j).wait_send()

        @pl.when((z < nz - 1) & (j < s_n - 1) & (j < tz * (z + 1)))
        def _():
            up(g, j).wait_send()

        across(g, j).wait_send()
        return carry

    lax.fori_loop(0, total, drain, 0)
    for g in range(NH):
        for d in range(1, nz):
            rs(g, d).wait_send()
            ag(g, d).wait_send()
        last(g).wait_send()
    reduce_4(h)


def solution(mesh):
    n_row, n_col = mesh.shape["prow"], mesh.shape["pcol"]
    nz = n_row // NY

    def per_device(ancestor_inverse, l_panel, diag_inverse, pattern):
        b = diag_inverse.shape[1]
        rt = l_panel.shape[0] // b
        nodes = l_panel.shape[1] // b
        na, s_n = rt * n_row, pattern.shape[1]
        share = rt // n_col
        bh = b // NH
        bf, f32 = jnp.bfloat16, jnp.float32
        slots = pltpu.VMEM((NH, s_n, b, bh), bf)
        sems = pltpu.SemaphoreType.DMA((NH, s_n))
        zsem = pltpu.SemaphoreType.DMA((NH, nz))
        half = pltpu.VMEM((NH, b, bh), f32)
        vmem = pl.BlockSpec(memory_space=pltpu.VMEM)
        return pl.pallas_call(
            functools.partial(kernel, (nz, rt, share, na, s_n, b)),
            out_shape=(jax.ShapeDtypeStruct(l_panel.shape, f32), jax.ShapeDtypeStruct(diag_inverse.shape, f32)),
            in_specs=[pl.BlockSpec(memory_space=pl.ANY), vmem, vmem, pl.BlockSpec(memory_space=pltpu.SMEM)],
            out_specs=(vmem, vmem),
            scratch_shapes=[
                pltpu.VMEM((n_col, na // n_col, rt * b, b), bf),
                pltpu.VMEM((NH, rt * NY, b, bh), bf),
                slots, slots, slots, slots, slots, slots,
                pltpu.VMEM((nodes, NH, rt * b, bh), f32),
                pltpu.VMEM((NH, nodes, b, bh), f32),
                half, half,
                pltpu.VMEM((NH, nz, b // nz, bh), f32),
                half, half,
                pltpu.SemaphoreType.DMA((3, na // n_col)),
                pltpu.SemaphoreType.DMA((NH, rt)),
                pltpu.SemaphoreType.DMA((NH, rt)),
                sems, sems, sems, sems, sems, sems,
                pltpu.SemaphoreType.DMA((NH, 4)),
                zsem, zsem, zsem, zsem,
            ],
            compiler_params=pltpu.CompilerParams(collective_id=0, has_side_effects=True, vmem_limit_bytes=56 * 2**20),
            cost_estimate=pl.CostEstimate(flops=4 * 10**9, bytes_accessed=2**23, transcendentals=0),
        )(ancestor_inverse, l_panel, diag_inverse, pattern)

    return jax.shard_map(
        per_device,
        mesh=mesh,
        in_specs=(P(("pole", "prow"), "pcol"), P(("pole", "prow"), "pcol"), P(("pole", "pcol"), None), P()),
        out_specs=(P(("pole", "prow"), "pcol"), P(("pole", "pcol"), None)),
        check_vma=False,
    )
```

```python
import functools

import jax
import jax.numpy as jnp
from jax import lax
from jax.experimental import pallas as pl
from jax.experimental.pallas import tpu as pltpu
from jax.sharding import PartitionSpec as P

MESH = pl.DeviceIdType.MESH
NY = 2
N_COL = 2
NH = 2
GAP = 3
SKEW = 4


def kernel(cfg, a_hbm, l_ref, d_ref, pat, out_ref, diag_ref, a_full, own, ubuf, dbuf, sd, su, fin, yin, acc,
           part, yr, ysum, zr, tot, ytot, a_sem, ph_ss, ph_rs, sd_ss, u_rs, su_ss, d_rs, fin_ss, y_rs, r_sem, zs_ss, zs_rs,
           zg_ss, zg_rs):
    nz, rt, share, na, s_n, b = cfg
    bh = b // NH
    tz = rt * NY
    row = lax.axis_index("prow")
    c = lax.axis_index("pcol")
    y = lax.rem(row, NY)
    z = row // NY
    oy = NY - 1 - y
    ypeer = {"prow": z * NY + oy}
    cpeer = {"pcol": 1 - c}

    def zdev(zz):
        return {"prow": zz * NY + y}

    barrier = pltpu.get_barrier_semaphore()
    pl.semaphore_signal(barrier, inc=1, device_id=ypeer, device_id_type=MESH)
    pl.semaphore_signal(barrier, inc=1, device_id=cpeer, device_id_type=MESH)
    for d in range(1, nz):
        pl.semaphore_signal(barrier, inc=1, device_id=zdev(lax.rem(z + d, nz)), device_id_type=MESH)
    acc[...] = jnp.zeros_like(acc)
    n_a = na // N_COL

    def a_local(i):
        return pltpu.make_async_copy(a_hbm.at[:, i * b:(i + 1) * b], a_full.at[c, i], a_sem.at[0, i])

    for i in range(n_a):
        a_local(i).start()
    pl.semaphore_wait(barrier, nz + 1)

    def remote(src, dst, ss, rs, dev):
        return pltpu.make_async_remote_copy(src_ref=src, dst_ref=dst, send_sem=ss, recv_sem=rs, device_id=dev,
                                            device_id_type=MESH)

    def a_send(i):
        return remote(a_hbm.at[:, i * b:(i + 1) * b], a_full.at[c, i], a_sem.at[1, i], a_sem.at[2, i], cpeer)

    def phase1(h, i):
        lanes = pl.ds(pl.multiple_of(oy * b + h * bh, 128), bh)
        return remote(l_ref.at[i * b:(i + 1) * b, lanes], own.at[h, y * rt + i], ph_ss.at[h, i], ph_rs.at[h, i], ypeer)

    for h in range(NH):
        for i in range(rt):
            phase1(h, i).start()
    for i in range(n_a):
        a_send(i).start()
    for h in range(NH):
        lanes = pl.ds(pl.multiple_of(y * b + h * bh, 128), bh)
        for i in range(rt):
            own[h, y * rt + i] = l_ref[i * b:(i + 1) * b, lanes]
    for i in range(rt):
        phase1(0, i).wait_recv()

    below = lax.rem(z + nz - 1, nz)
    above = lax.rem(z + 1, nz)

    def down(h, j):
        return remote(sd.at[h, j], ubuf.at[h, j], sd_ss.at[h, j], u_rs.at[h, j], zdev(below))

    def up(h, j):
        return remote(su.at[h, j], dbuf.at[h, j], su_ss.at[h, j], d_rs.at[h, j], zdev(above))

    def across(h, j):
        return remote(fin.at[h, j], yin.at[h, j], fin_ss.at[h, j], y_rs.at[h, j], ypeer)

    nodes = l_ref.shape[1] // b
    zc = min((na - s_n) // tz, nz - 1)
    j0 = jnp.maximum(tz * z - (na - s_n), 0)
    lag_d = SKEW * jnp.maximum(zc - z, 0)
    lag_u = SKEW * z
    lag_f = jnp.maximum(lag_d, lag_u)
    total = NH * s_n

    def tile_of(k, j):
        return pat[c * nodes + k, j]

    def own_tile(h, t):
        v = own[h, 0]
        for i in range(1, tz):
            v = lax.select(t == tz * z + i, own[h, i], v)
        return v

    def a_tile(t):
        part_at = lax.rem(t, rt) // share
        li = (t // rt) * share + lax.rem(t, share)
        return a_full[part_at, li]

    ch = b // nz
    at_y = pl.ds(pl.multiple_of(y * b, 8), b)
    at_o = pl.ds(pl.multiple_of(oy * b, 8), b)
    mine = pl.ds(pl.multiple_of(z * ch, 8), ch)

    def first(h):
        return remote(part.at[h, oy], yr.at[h], r_sem.at[h, 0], r_sem.at[h, 1], ypeer)

    def last(h):
        return remote(tot.at[h], ytot.at[h], r_sem.at[h, 2], r_sem.at[h, 3], ypeer)

    def rs(h, d):
        to = lax.rem(z + d, nz)
        return remote(ysum.at[h, pl.ds(pl.multiple_of(to * ch, 8), ch), :], zr.at[h, d], zs_ss.at[h, d],
                      zs_rs.at[h, d], zdev(to))

    def ag(h, d):
        to = lax.rem(z + d, nz)
        return remote(tot.at[h, mine, :], tot.at[h, mine, :], zg_ss.at[h, d], zg_rs.at[h, d], zdev(to))

    def ag_in(h, d):
        at = lax.rem(z + nz - d, nz)
        there = pl.ds(pl.multiple_of(at * ch, 8), ch)
        return remote(tot.at[h, there, :], tot.at[h, there, :], zg_ss.at[h, d], zg_rs.at[h, d], zdev(at))

    def reduce_0(h):
        for k in range(nodes):
            at = slice(k * b + h * bh, k * b + (h + 1) * bh)
            for i in range(rt):
                t = row * rt + i
                hit = pat[c * nodes + k, 0] == t
                for j in range(1, s_n):
                    hit = hit | (pat[c * nodes + k, j] == t)
                m = -jnp.where(hit, 1.0, 0.0).astype(jnp.float32)
                out_ref[i * b:(i + 1) * b, at] = acc[k, h, i * b:(i + 1) * b, :] * m
            x = out_ref[:, at]
            hi = x.astype(jnp.bfloat16)
            lo = (x - hi.astype(jnp.float32)).astype(jnp.bfloat16)
            both = lax.dot_general(l_ref[:, k * b:(k + 1) * b], jnp.concatenate([hi, lo], axis=1),
                                   (((0,), (0,)), ((), ())), preferred_element_type=jnp.float32)
            part[h, k] = both[:, :bh] + both[:, bh:]
        first(h).start()

    def reduce_1(h):
        first(h).wait()
        ysum[h] = part[h, y] + yr[h]
        for d in range(1, nz):
            rs(h, d).start()

    def reduce_2(h):
        total_z = ysum[h, mine, :]
        for d in range(1, nz):
            rs(h, d).wait_recv()
            total_z = total_z + zr[h, d]
        tot[h, mine, :] = total_z
        for d in range(1, nz):
            ag(h, d).start()

    def reduce_3(h):
        for d in range(1, nz):
            ag_in(h, d).wait_recv()
        last(h).start()
        lanes = slice(h * bh, (h + 1) * bh)
        diag_ref[at_y, lanes] = d_ref[at_y, lanes] - tot[h]

    def reduce_4(h):
        lanes = slice(h * bh, (h + 1) * bh)
        last(h).wait_recv()
        diag_ref[at_o, lanes] = d_ref[at_o, lanes] - ytot[h]

    def step(s, carry):
        @pl.when(s == s_n)
        def _():
            for h in range(1, NH):
                for i in range(rt):
                    phase1(h, i).wait_recv()

        @pl.when(s == lag_f)
        def _():
            for i in range(n_a):
                a_local(i).wait()
                a_send(i).wait()

        pd = s - lag_d
        hd, jd = pd // s_n, j0 + lax.rem(pd, s_n)
        live = (pd >= 0) & (pd < total) & (jd < s_n)

        @pl.when(live & (z < nz - 1) & (jd + (na - s_n) >= tz * (z + 1)))
        def _():
            down(hd, jd).wait_recv()

        @pl.when(live & (z > 0))
        def _():
            t = tile_of(y, jd)
            sd[hd, jd] = lax.select(t < tz * (z + 1), own_tile(hd, t), ubuf[hd, jd])
            down(hd, jd).start()

        pu = s - lag_u
        hu, ju = pu // s_n, lax.rem(pu, s_n)
        live_u = (pu >= 0) & (pu < total) & (ju < s_n - 1)

        @pl.when(live_u & (z > 0) & (ju < tz * z))
        def _():
            up(hu, ju).wait_recv()

        @pl.when(live_u & (z < nz - 1) & (ju < tz * (z + 1)))
        def _():
            t = tile_of(y, ju)
            su[hu, ju] = lax.select(t >= tz * z, own_tile(hu, t), dbuf[hu, ju])
            up(hu, ju).start()

        pf = s - lag_f
        hf, jf = pf // s_n, lax.rem(pf, s_n)

        @pl.when((pf >= 0) & (pf < total))
        def _():
            t = tile_of(y, jf)
            v = lax.select(t < tz * z, dbuf[hf, jf], own_tile(hf, t))
            v = lax.select(t >= tz * (z + 1), ubuf[hf, jf], v)
            fin[hf, jf] = v
            across(hf, jf).start()
            acc[y, hf] += jnp.dot(a_tile(t), v, preferred_element_type=jnp.float32)

        py = pf - SKEW
        hy, jy = py // s_n, lax.rem(py, s_n)

        @pl.when((py >= 0) & (py < total))
        def _():
            across(hy, jy).wait_recv()
            t = tile_of(oy, jy)
            acc[oy, hy] += jnp.dot(a_tile(t), yin[hy, jy], preferred_element_type=jnp.float32)

        for h in range(NH - 1):
            done = (h + 1) * s_n + SKEW

            @pl.when(s == done + lag_f)
            def _(h=h):
                reduce_0(h)

            @pl.when(s == done + lag_f + GAP)
            def _(h=h):
                reduce_1(h)

            @pl.when(s == done + SKEW * (nz - 1) + 2 * GAP)
            def _(h=h):
                reduce_2(h)

        return carry

    lax.fori_loop(0, total + SKEW * nz, step, 0)

    for h in range(NH - 1):
        reduce_3(h)
    h = NH - 1
    reduce_0(h)
    for g in range(NH - 1):
        reduce_4(g)
    reduce_1(h)
    reduce_2(h)
    reduce_3(h)

    for g in range(NH):
        for i in range(rt):
            phase1(g, i).wait_send()

    def drain(p, carry):
        g, j = p // s_n, lax.rem(p, s_n)

        @pl.when((z > 0) & (j >= j0))
        def _():
            down(g, j).wait_send()

        @pl.when((z < nz - 1) & (j < s_n - 1) & (j < tz * (z + 1)))
        def _():
            up(g, j).wait_send()

        across(g, j).wait_send()
        return carry

    lax.fori_loop(0, total, drain, 0)
    for g in range(NH):
        for d in range(1, nz):
            rs(g, d).wait_send()
            ag(g, d).wait_send()
        last(g).wait_send()
    reduce_4(h)


def solution(mesh):
    n_row, n_col = mesh.shape["prow"], mesh.shape["pcol"]
    nz = n_row // NY

    def per_device(ancestor_inverse, l_panel, diag_inverse, pattern):
        b = diag_inverse.shape[1]
        rt = l_panel.shape[0] // b
        nodes = l_panel.shape[1] // b
        na, s_n = rt * n_row, pattern.shape[1]
        share = rt // n_col
        bh = b // NH
        bf, f32 = jnp.bfloat16, jnp.float32
        slots = pltpu.VMEM((NH, s_n, b, bh), bf)
        sems = pltpu.SemaphoreType.DMA((NH, s_n))
        zsem = pltpu.SemaphoreType.DMA((NH, nz))
        half = pltpu.VMEM((NH, b, bh), f32)
        vmem = pl.BlockSpec(memory_space=pltpu.VMEM)
        return pl.pallas_call(
            functools.partial(kernel, (nz, rt, share, na, s_n, b)),
            out_shape=(jax.ShapeDtypeStruct(l_panel.shape, f32), jax.ShapeDtypeStruct(diag_inverse.shape, f32)),
            in_specs=[pl.BlockSpec(memory_space=pl.ANY), vmem, vmem, pl.BlockSpec(memory_space=pltpu.SMEM)],
            out_specs=(vmem, vmem),
            scratch_shapes=[
                pltpu.VMEM((n_col, na // n_col, rt * b, b), bf),
                pltpu.VMEM((NH, rt * NY, b, bh), bf),
                slots, slots, slots, slots, slots, slots,
                pltpu.VMEM((nodes, NH, rt * b, bh), f32),
                pltpu.VMEM((NH, nodes, b, bh), f32),
                half, half,
                pltpu.VMEM((NH, nz, b // nz, bh), f32),
                half, half,
                pltpu.SemaphoreType.DMA((3, na // n_col)),
                pltpu.SemaphoreType.DMA((NH, rt)),
                pltpu.SemaphoreType.DMA((NH, rt)),
                sems, sems, sems, sems, sems, sems,
                pltpu.SemaphoreType.DMA((NH, 4)),
                zsem, zsem, zsem, zsem,
            ],
            compiler_params=pltpu.CompilerParams(collective_id=0, has_side_effects=True, vmem_limit_bytes=56 * 2**20),
            cost_estimate=pl.CostEstimate(flops=4 * 10**9, bytes_accessed=2**23, transcendentals=0),
        )(ancestor_inverse, l_panel, diag_inverse, pattern)

    return jax.shard_map(
        per_device,
        mesh=mesh,
        in_specs=(P(("pole", "prow"), "pcol"), P(("pole", "prow"), "pcol"), P(("pole", "pcol"), None), P()),
        out_specs=(P(("pole", "prow"), "pcol"), P(("pole", "pcol"), None)),
        check_vma=False,
    )
```

```python
import functools

import jax
import jax.numpy as jnp
from jax import lax
from jax.experimental import pallas as pl
from jax.experimental.pallas import tpu as pltpu
from jax.sharding import PartitionSpec as P

MESH = pl.DeviceIdType.MESH
NY = 2
N_COL = 2
NH = 1
GAP = 3
SKEW = 2


def kernel(cfg, a_hbm, l_ref, d_ref, pat, out_ref, diag_ref, a_full, own, ubuf, dbuf, sd, su, fin, yin, acc,
           part, yr, ysum, zr, tot, ytot, a_sem, ph_ss, ph_rs, sd_ss, u_rs, su_ss, d_rs, fin_ss, y_rs, r_sem, zs_ss, zs_rs,
           zg_ss, zg_rs):
    nz, rt, share, na, s_n, b = cfg
    bh = b // NH
    tz = rt * NY
    row = lax.axis_index("prow")
    c = lax.axis_index("pcol")
    y = lax.rem(row, NY)
    z = row // NY
    oy = NY - 1 - y
    ypeer = {"prow": z * NY + oy}
    cpeer = {"pcol": 1 - c}

    def zdev(zz):
        return {"prow": zz * NY + y}

    barrier = pltpu.get_barrier_semaphore()
    pl.semaphore_signal(barrier, inc=1, device_id=ypeer, device_id_type=MESH)
    pl.semaphore_signal(barrier, inc=1, device_id=cpeer, device_id_type=MESH)
    for d in range(1, nz):
        pl.semaphore_signal(barrier, inc=1, device_id=zdev(lax.rem(z + d, nz)), device_id_type=MESH)
    acc[...] = jnp.zeros_like(acc)
    n_a = na // N_COL

    def a_local(i):
        return pltpu.make_async_copy(a_hbm.at[:, i * b:(i + 1) * b], a_full.at[c, i], a_sem.at[0, i])

    for i in range(n_a):
        a_local(i).start()
    pl.semaphore_wait(barrier, nz + 1)

    def remote(src, dst, ss, rs, dev):
        return pltpu.make_async_remote_copy(src_ref=src, dst_ref=dst, send_sem=ss, recv_sem=rs, device_id=dev,
                                            device_id_type=MESH)

    def a_send(i):
        return remote(a_hbm.at[:, i * b:(i + 1) * b], a_full.at[c, i], a_sem.at[1, i], a_sem.at[2, i], cpeer)

    def phase1(h, i):
        lanes = pl.ds(pl.multiple_of(oy * b + h * bh, 128), bh)
        return remote(l_ref.at[i * b:(i + 1) * b, lanes], own.at[h, y * rt + i], ph_ss.at[h, i], ph_rs.at[h, i], ypeer)

    for h in range(NH):
        for i in range(rt):
            phase1(h, i).start()
    for i in range(n_a):
        a_send(i).start()
    for h in range(NH):
        lanes = pl.ds(pl.multiple_of(y * b + h * bh, 128), bh)
        for i in range(rt):
            own[h, y * rt + i] = l_ref[i * b:(i + 1) * b, lanes]
    for i in range(rt):
        phase1(0, i).wait_recv()

    below = lax.rem(z + nz - 1, nz)
    above = lax.rem(z + 1, nz)

    def down(h, j):
        return remote(sd.at[h, j], ubuf.at[h, j], sd_ss.at[h, j], u_rs.at[h, j], zdev(below))

    def up(h, j):
        return remote(su.at[h, j], dbuf.at[h, j], su_ss.at[h, j], d_rs.at[h, j], zdev(above))

    def across(h, j):
        return remote(fin.at[h, j], yin.at[h, j], fin_ss.at[h, j], y_rs.at[h, j], ypeer)

    nodes = l_ref.shape[1] // b
    zc = min((na - s_n) // tz, nz - 1)
    j0 = jnp.maximum(tz * z - (na - s_n), 0)
    lag_d = SKEW * jnp.maximum(zc - z, 0)
    lag_u = SKEW * z
    lag_f = jnp.maximum(lag_d, lag_u)
    total = NH * s_n

    def tile_of(k, j):
        return pat[c * nodes + k, j]

    def own_tile(h, t):
        v = own[h, 0]
        for i in range(1, tz):
            v = lax.select(t == tz * z + i, own[h, i], v)
        return v

    def a_tile(t):
        part_at = lax.rem(t, rt) // share
        li = (t // rt) * share + lax.rem(t, share)
        return a_full[part_at, li]

    ch = b // nz
    at_y = pl.ds(pl.multiple_of(y * b, 8), b)
    at_o = pl.ds(pl.multiple_of(oy * b, 8), b)
    mine = pl.ds(pl.multiple_of(z * ch, 8), ch)

    def first(h):
        return remote(part.at[h, oy], yr.at[h], r_sem.at[h, 0], r_sem.at[h, 1], ypeer)

    def last(h):
        return remote(tot.at[h], ytot.at[h], r_sem.at[h, 2], r_sem.at[h, 3], ypeer)

    def rs(h, d):
        to = lax.rem(z + d, nz)
        return remote(ysum.at[h, pl.ds(pl.multiple_of(to * ch, 8), ch), :], zr.at[h, d], zs_ss.at[h, d],
                      zs_rs.at[h, d], zdev(to))

    def ag(h, d):
        to = lax.rem(z + d, nz)
        return remote(tot.at[h, mine, :], tot.at[h, mine, :], zg_ss.at[h, d], zg_rs.at[h, d], zdev(to))

    def ag_in(h, d):
        at = lax.rem(z + nz - d, nz)
        there = pl.ds(pl.multiple_of(at * ch, 8), ch)
        return remote(tot.at[h, there, :], tot.at[h, there, :], zg_ss.at[h, d], zg_rs.at[h, d], zdev(at))

    def reduce_0(h):
        for k in range(nodes):
            at = slice(k * b + h * bh, k * b + (h + 1) * bh)
            for i in range(rt):
                t = row * rt + i
                hit = pat[c * nodes + k, 0] == t
                for j in range(1, s_n):
                    hit = hit | (pat[c * nodes + k, j] == t)
                m = -jnp.where(hit, 1.0, 0.0).astype(jnp.float32)
                out_ref[i * b:(i + 1) * b, at] = acc[k, h, i * b:(i + 1) * b, :] * m
            x = out_ref[:, at]
            hi = x.astype(jnp.bfloat16)
            lo = (x - hi.astype(jnp.float32)).astype(jnp.bfloat16)
            both = lax.dot_general(l_ref[:, k * b:(k + 1) * b], jnp.concatenate([hi, lo], axis=1),
                                   (((0,), (0,)), ((), ())), preferred_element_type=jnp.float32)
            part[h, k] = both[:, :bh] + both[:, bh:]
        first(h).start()

    def reduce_1(h):
        first(h).wait()
        ysum[h] = part[h, y] + yr[h]
        for d in range(1, nz):
            rs(h, d).start()

    def reduce_2(h):
        total_z = ysum[h, mine, :]
        for d in range(1, nz):
            rs(h, d).wait_recv()
            total_z = total_z + zr[h, d]
        tot[h, mine, :] = total_z
        for d in range(1, nz):
            ag(h, d).start()

    def reduce_3(h):
        for d in range(1, nz):
            ag_in(h, d).wait_recv()
        last(h).start()
        lanes = slice(h * bh, (h + 1) * bh)
        diag_ref[at_y, lanes] = d_ref[at_y, lanes] - tot[h]

    def reduce_4(h):
        lanes = slice(h * bh, (h + 1) * bh)
        last(h).wait_recv()
        diag_ref[at_o, lanes] = d_ref[at_o, lanes] - ytot[h]

    def step(s, carry):
        @pl.when(s == s_n)
        def _():
            for h in range(1, NH):
                for i in range(rt):
                    phase1(h, i).wait_recv()

        @pl.when(s == lag_f)
        def _():
            for i in range(n_a):
                a_local(i).wait()
                a_send(i).wait()

        pd = s - lag_d
        hd, jd = pd // s_n, j0 + lax.rem(pd, s_n)
        live = (pd >= 0) & (pd < total) & (jd < s_n)

        @pl.when(live & (z < nz - 1) & (jd + (na - s_n) >= tz * (z + 1)))
        def _():
            down(hd, jd).wait_recv()

        @pl.when(live & (z > 0))
        def _():
            t = tile_of(y, jd)
            sd[hd, jd] = lax.select(t < tz * (z + 1), own_tile(hd, t), ubuf[hd, jd])
            down(hd, jd).start()

        pu = s - lag_u
        hu, ju = pu // s_n, lax.rem(pu, s_n)
        live_u = (pu >= 0) & (pu < total) & (ju < s_n - 1)

        @pl.when(live_u & (z > 0) & (ju < tz * z))
        def _():
            up(hu, ju).wait_recv()

        @pl.when(live_u & (z < nz - 1) & (ju < tz * (z + 1)))
        def _():
            t = tile_of(y, ju)
            su[hu, ju] = lax.select(t >= tz * z, own_tile(hu, t), dbuf[hu, ju])
            up(hu, ju).start()

        pf = s - lag_f
        hf, jf = pf // s_n, lax.rem(pf, s_n)

        @pl.when((pf >= 0) & (pf < total))
        def _():
            t = tile_of(y, jf)
            v = lax.select(t < tz * z, dbuf[hf, jf], own_tile(hf, t))
            v = lax.select(t >= tz * (z + 1), ubuf[hf, jf], v)
            fin[hf, jf] = v
            across(hf, jf).start()
            acc[y, hf] += jnp.dot(a_tile(t), v, preferred_element_type=jnp.float32)

        py = pf - SKEW
        hy, jy = py // s_n, lax.rem(py, s_n)

        @pl.when((py >= 0) & (py < total))
        def _():
            across(hy, jy).wait_recv()
            t = tile_of(oy, jy)
            acc[oy, hy] += jnp.dot(a_tile(t), yin[hy, jy], preferred_element_type=jnp.float32)

        for h in range(NH - 1):
            done = (h + 1) * s_n + SKEW

            @pl.when(s == done + lag_f)
            def _(h=h):
                reduce_0(h)

            @pl.when(s == done + lag_f + GAP)
            def _(h=h):
                reduce_1(h)

            @pl.when(s == done + SKEW * (nz - 1) + 2 * GAP)
            def _(h=h):
                reduce_2(h)

        return carry

    lax.fori_loop(0, total + SKEW * nz, step, 0)

    for h in range(NH - 1):
        reduce_3(h)
    h = NH - 1
    reduce_0(h)
    for g in range(NH - 1):
        reduce_4(g)
    reduce_1(h)
    reduce_2(h)
    reduce_3(h)

    for g in range(NH):
        for i in range(rt):
            phase1(g, i).wait_send()

    def drain(p, carry):
        g, j = p // s_n, lax.rem(p, s_n)

        @pl.when((z > 0) & (j >= j0))
        def _():
            down(g, j).wait_send()

        @pl.when((z < nz - 1) & (j < s_n - 1) & (j < tz * (z + 1)))
        def _():
            up(g, j).wait_send()

        across(g, j).wait_send()
        return carry

    lax.fori_loop(0, total, drain, 0)
    for g in range(NH):
        for d in range(1, nz):
            rs(g, d).wait_send()
            ag(g, d).wait_send()
        last(g).wait_send()
    reduce_4(h)


def solution(mesh):
    n_row, n_col = mesh.shape["prow"], mesh.shape["pcol"]
    nz = n_row // NY

    def per_device(ancestor_inverse, l_panel, diag_inverse, pattern):
        b = diag_inverse.shape[1]
        rt = l_panel.shape[0] // b
        nodes = l_panel.shape[1] // b
        na, s_n = rt * n_row, pattern.shape[1]
        share = rt // n_col
        bh = b // NH
        bf, f32 = jnp.bfloat16, jnp.float32
        slots = pltpu.VMEM((NH, s_n, b, bh), bf)
        sems = pltpu.SemaphoreType.DMA((NH, s_n))
        zsem = pltpu.SemaphoreType.DMA((NH, nz))
        half = pltpu.VMEM((NH, b, bh), f32)
        vmem = pl.BlockSpec(memory_space=pltpu.VMEM)
        return pl.pallas_call(
            functools.partial(kernel, (nz, rt, share, na, s_n, b)),
            out_shape=(jax.ShapeDtypeStruct(l_panel.shape, f32), jax.ShapeDtypeStruct(diag_inverse.shape, f32)),
            in_specs=[pl.BlockSpec(memory_space=pl.ANY), vmem, vmem, pl.BlockSpec(memory_space=pltpu.SMEM)],
            out_specs=(vmem, vmem),
            scratch_shapes=[
                pltpu.VMEM((n_col, na // n_col, rt * b, b), bf),
                pltpu.VMEM((NH, rt * NY, b, bh), bf),
                slots, slots, slots, slots, slots, slots,
                pltpu.VMEM((nodes, NH, rt * b, bh), f32),
                pltpu.VMEM((NH, nodes, b, bh), f32),
                half, half,
                pltpu.VMEM((NH, nz, b // nz, bh), f32),
                half, half,
                pltpu.SemaphoreType.DMA((3, na // n_col)),
                pltpu.SemaphoreType.DMA((NH, rt)),
                pltpu.SemaphoreType.DMA((NH, rt)),
                sems, sems, sems, sems, sems, sems,
                pltpu.SemaphoreType.DMA((NH, 4)),
                zsem, zsem, zsem, zsem,
            ],
            compiler_params=pltpu.CompilerParams(collective_id=0, has_side_effects=True, vmem_limit_bytes=56 * 2**20),
            cost_estimate=pl.CostEstimate(flops=4 * 10**9, bytes_accessed=2**23, transcendentals=0),
        )(ancestor_inverse, l_panel, diag_inverse, pattern)

    return jax.shard_map(
        per_device,
        mesh=mesh,
        in_specs=(P(("pole", "prow"), "pcol"), P(("pole", "prow"), "pcol"), P(("pole", "pcol"), None), P()),
        out_specs=(P(("pole", "prow"), "pcol"), P(("pole", "pcol"), None)),
        check_vma=False,
    )
```

```python
import functools

import jax
import jax.numpy as jnp
from jax import lax
from jax.experimental import pallas as pl
from jax.experimental.pallas import tpu as pltpu
from jax.sharding import PartitionSpec as P

MESH = pl.DeviceIdType.MESH
NY = 2
N_COL = 2
NH = 2
GAP = 3
SKEW = 3


def kernel(cfg, a_hbm, l_ref, d_ref, pat, out_ref, diag_ref, a_full, own, ubuf, dbuf, sd, su, fin, yin, acc,
           part, yr, ysum, zr, tot, ytot, a_sem, ph_ss, ph_rs, sd_ss, u_rs, su_ss, d_rs, fin_ss, y_rs, r_sem, zs_ss, zs_rs,
           zg_ss, zg_rs):
    nz, rt, share, na, s_n, b = cfg
    bh = b // NH
    tz = rt * NY
    row = lax.axis_index("prow")
    c = lax.axis_index("pcol")
    y = lax.rem(row, NY)
    z = row // NY
    oy = NY - 1 - y
    ypeer = {"prow": z * NY + oy}
    cpeer = {"pcol": 1 - c}

    def zdev(zz):
        return {"prow": zz * NY + y}

    barrier = pltpu.get_barrier_semaphore()
    pl.semaphore_signal(barrier, inc=1, device_id=ypeer, device_id_type=MESH)
    pl.semaphore_signal(barrier, inc=1, device_id=cpeer, device_id_type=MESH)
    for d in range(1, nz):
        pl.semaphore_signal(barrier, inc=1, device_id=zdev(lax.rem(z + d, nz)), device_id_type=MESH)
    acc[...] = jnp.zeros_like(acc)
    n_a = na // N_COL

    def a_local(i):
        return pltpu.make_async_copy(a_hbm.at[:, i * b:(i + 1) * b], a_full.at[c, i], a_sem.at[0, i])

    for i in range(n_a):
        a_local(i).start()
    pl.semaphore_wait(barrier, nz + 1)

    def remote(src, dst, ss, rs, dev):
        return pltpu.make_async_remote_copy(src_ref=src, dst_ref=dst, send_sem=ss, recv_sem=rs, device_id=dev,
                                            device_id_type=MESH)

    def a_send(i):
        cols = pl.ds(pl.multiple_of(i * b, 128), b)
        return remote(a_hbm.at[:, cols], a_full.at[c, i], a_sem.at[1, i], a_sem.at[2, i], cpeer)

    def phase1(h, i):
        lanes = pl.ds(pl.multiple_of(oy * b + h * bh, 128), bh)
        return remote(l_ref.at[i * b:(i + 1) * b, lanes], own.at[h, y * rt + i], ph_ss.at[h, i], ph_rs.at[h, i], ypeer)

    for h in range(NH):
        for i in range(rt):
            phase1(h, i).start()
    for h in range(NH):
        lanes = pl.ds(pl.multiple_of(y * b + h * bh, 128), bh)
        for i in range(rt):
            own[h, y * rt + i] = l_ref[i * b:(i + 1) * b, lanes]
    for i in range(rt):
        phase1(0, i).wait_recv()

    below = lax.rem(z + nz - 1, nz)
    above = lax.rem(z + 1, nz)

    def down(h, j):
        return remote(sd.at[h, j], ubuf.at[h, j], sd_ss.at[h, j], u_rs.at[h, j], zdev(below))

    def up(h, j):
        return remote(su.at[h, j], dbuf.at[h, j], su_ss.at[h, j], d_rs.at[h, j], zdev(above))

    def across(h, j):
        return remote(fin.at[h, j], yin.at[h, j], fin_ss.at[h, j], y_rs.at[h, j], ypeer)

    nodes = l_ref.shape[1] // b
    zc = min((na - s_n) // tz, nz - 1)
    j0 = jnp.maximum(tz * z - (na - s_n), 0)
    lag_d = SKEW * jnp.maximum(zc - z, 0)
    lag_u = SKEW * z
    lag_f = jnp.maximum(lag_d, lag_u)
    total = NH * s_n

    def tile_of(k, j):
        return pat[c * nodes + k, j]

    def own_tile(h, t):
        v = own[h, 0]
        for i in range(1, tz):
            v = lax.select(t == tz * z + i, own[h, i], v)
        return v

    def a_tile(t):
        part_at = lax.rem(t, rt) // share
        li = (t // rt) * share + lax.rem(t, share)
        return a_full[part_at, li]

    def bulk(k, src):
        def one(j, carry):
            acc[k, 0] += jnp.dot(a_tile(tile_of(k, j)), src[0, j], preferred_element_type=jnp.float32)
            return carry

        lax.fori_loop(0, s_n, one, 0)

    ch = b // nz
    at_y = pl.ds(pl.multiple_of(y * b, 8), b)
    at_o = pl.ds(pl.multiple_of(oy * b, 8), b)
    mine = pl.ds(pl.multiple_of(z * ch, 8), ch)

    def first(h):
        return remote(part.at[h, oy], yr.at[h], r_sem.at[h, 0], r_sem.at[h, 1], ypeer)

    def last(h):
        return remote(tot.at[h], ytot.at[h], r_sem.at[h, 2], r_sem.at[h, 3], ypeer)

    def rs(h, d):
        to = lax.rem(z + d, nz)
        return remote(ysum.at[h, pl.ds(pl.multiple_of(to * ch, 8), ch), :], zr.at[h, d], zs_ss.at[h, d],
                      zs_rs.at[h, d], zdev(to))

    def ag(h, d):
        to = lax.rem(z + d, nz)
        return remote(tot.at[h, mine, :], tot.at[h, mine, :], zg_ss.at[h, d], zg_rs.at[h, d], zdev(to))

    def ag_in(h, d):
        at = lax.rem(z + nz - d, nz)
        there = pl.ds(pl.multiple_of(at * ch, 8), ch)
        return remote(tot.at[h, there, :], tot.at[h, there, :], zg_ss.at[h, d], zg_rs.at[h, d], zdev(at))

    def reduce_0(h):
        for k in range(nodes):
            at = slice(k * b + h * bh, k * b + (h + 1) * bh)
            for i in range(rt):
                t = row * rt + i
                hit = pat[c * nodes + k, 0] == t
                for j in range(1, s_n):
                    hit = hit | (pat[c * nodes + k, j] == t)
                m = -jnp.where(hit, 1.0, 0.0).astype(jnp.float32)
                out_ref[i * b:(i + 1) * b, at] = acc[k, h, i * b:(i + 1) * b, :] * m
            x = out_ref[:, at]
            hi = x.astype(jnp.bfloat16)
            lo = (x - hi.astype(jnp.float32)).astype(jnp.bfloat16)
            both = lax.dot_general(l_ref[:, k * b:(k + 1) * b], jnp.concatenate([hi, lo], axis=1),
                                   (((0,), (0,)), ((), ())), preferred_element_type=jnp.float32)
            part[h, k] = both[:, :bh] + both[:, bh:]
        first(h).start()

    def reduce_1(h):
        first(h).wait()
        ysum[h] = part[h, y] + yr[h]
        for d in range(1, nz):
            rs(h, d).start()

    def reduce_2(h):
        total_z = ysum[h, mine, :]
        for d in range(1, nz):
            rs(h, d).wait_recv()
            total_z = total_z + zr[h, d]
        tot[h, mine, :] = total_z
        for d in range(1, nz):
            ag(h, d).start()

    def reduce_3(h):
        for d in range(1, nz):
            ag_in(h, d).wait_recv()
        last(h).start()
        lanes = slice(h * bh, (h + 1) * bh)
        diag_ref[at_y, lanes] = d_ref[at_y, lanes] - tot[h]

    def reduce_4(h):
        lanes = slice(h * bh, (h + 1) * bh)
        last(h).wait_recv()
        diag_ref[at_o, lanes] = d_ref[at_o, lanes] - ytot[h]

    def step(s, carry):
        @pl.when(s == s_n)
        def _():
            for h in range(1, NH):
                for i in range(rt):
                    phase1(h, i).wait_recv()

        @pl.when(s == s_n + lag_f)
        def _():
            for i in range(n_a):
                a_local(i).wait()
                a_send(i).wait()

        pd = s - lag_d
        hd, jd = pd // s_n, j0 + lax.rem(pd, s_n)
        live = (pd >= 0) & (pd < total) & (jd < s_n)

        @pl.when(live & (z < nz - 1) & (jd + (na - s_n) >= tz * (z + 1)))
        def _():
            down(hd, jd).wait_recv()

        @pl.when(live & (z > 0))
        def _():
            t = tile_of(y, jd)
            sd[hd, jd] = lax.select(t < tz * (z + 1), own_tile(hd, t), ubuf[hd, jd])
            down(hd, jd).start()

        pu = s - lag_u
        hu, ju = pu // s_n, lax.rem(pu, s_n)
        live_u = (pu >= 0) & (pu < total) & (ju < s_n - 1)

        @pl.when(live_u & (z > 0) & (ju < tz * z))
        def _():
            up(hu, ju).wait_recv()

        @pl.when(live_u & (z < nz - 1) & (ju < tz * (z + 1)))
        def _():
            t = tile_of(y, ju)
            su[hu, ju] = lax.select(t >= tz * z, own_tile(hu, t), dbuf[hu, ju])
            up(hu, ju).start()

        pf = s - lag_f
        hf, jf = pf // s_n, lax.rem(pf, s_n)

        @pl.when((pf >= 0) & (pf < total))
        def _():
            t = tile_of(y, jf)
            v = lax.select(t < tz * z, dbuf[hf, jf], own_tile(hf, t))
            v = lax.select(t >= tz * (z + 1), ubuf[hf, jf], v)
            fin[hf, jf] = v
            across(hf, jf).start()

            @pl.when(hf > 0)
            def _():
                acc[y, hf] += jnp.dot(a_tile(t), v, preferred_element_type=jnp.float32)

        @pl.when(pf == s_n)
        def _():
            bulk(y, fin)

        py = pf - SKEW
        hy, jy = py // s_n, lax.rem(py, s_n)

        @pl.when((py >= 0) & (py < total))
        def _():
            across(hy, jy).wait_recv()
            t = tile_of(oy, jy)

            @pl.when(hy > 0)
            def _():
                acc[oy, hy] += jnp.dot(a_tile(t), yin[hy, jy], preferred_element_type=jnp.float32)

        @pl.when(py == s_n)
        def _():
            bulk(oy, yin)

        @pl.when(s < n_a)
        def _():
            a_send(s).start()

        for h in range(NH - 1):
            done = (h + 1) * s_n + SKEW

            @pl.when(s == done + lag_f)
            def _(h=h):
                reduce_0(h)

            @pl.when(s == done + lag_f + GAP)
            def _(h=h):
                reduce_1(h)

            @pl.when(s == done + SKEW * (nz - 1) + 2 * GAP)
            def _(h=h):
                reduce_2(h)

        return carry

    lax.fori_loop(0, total + SKEW * nz, step, 0)

    for h in range(NH - 1):
        reduce_3(h)
    h = NH - 1
    reduce_0(h)
    for g in range(NH - 1):
        reduce_4(g)
    reduce_1(h)
    reduce_2(h)
    reduce_3(h)

    for g in range(NH):
        for i in range(rt):
            phase1(g, i).wait_send()

    def drain(p, carry):
        g, j = p // s_n, lax.rem(p, s_n)

        @pl.when((z > 0) & (j >= j0))
        def _():
            down(g, j).wait_send()

        @pl.when((z < nz - 1) & (j < s_n - 1) & (j < tz * (z + 1)))
        def _():
            up(g, j).wait_send()

        across(g, j).wait_send()
        return carry

    lax.fori_loop(0, total, drain, 0)
    for g in range(NH):
        for d in range(1, nz):
            rs(g, d).wait_send()
            ag(g, d).wait_send()
        last(g).wait_send()
    reduce_4(h)


def solution(mesh):
    n_row, n_col = mesh.shape["prow"], mesh.shape["pcol"]
    nz = n_row // NY

    def per_device(ancestor_inverse, l_panel, diag_inverse, pattern):
        b = diag_inverse.shape[1]
        rt = l_panel.shape[0] // b
        nodes = l_panel.shape[1] // b
        na, s_n = rt * n_row, pattern.shape[1]
        share = rt // n_col
        bh = b // NH
        bf, f32 = jnp.bfloat16, jnp.float32
        slots = pltpu.VMEM((NH, s_n, b, bh), bf)
        sems = pltpu.SemaphoreType.DMA((NH, s_n))
        zsem = pltpu.SemaphoreType.DMA((NH, nz))
        half = pltpu.VMEM((NH, b, bh), f32)
        vmem = pl.BlockSpec(memory_space=pltpu.VMEM)
        return pl.pallas_call(
            functools.partial(kernel, (nz, rt, share, na, s_n, b)),
            out_shape=(jax.ShapeDtypeStruct(l_panel.shape, f32), jax.ShapeDtypeStruct(diag_inverse.shape, f32)),
            in_specs=[pl.BlockSpec(memory_space=pl.ANY), vmem, vmem, pl.BlockSpec(memory_space=pltpu.SMEM)],
            out_specs=(vmem, vmem),
            scratch_shapes=[
                pltpu.VMEM((n_col, na // n_col, rt * b, b), bf),
                pltpu.VMEM((NH, rt * NY, b, bh), bf),
                slots, slots, slots, slots, slots, slots,
                pltpu.VMEM((nodes, NH, rt * b, bh), f32),
                pltpu.VMEM((NH, nodes, b, bh), f32),
                half, half,
                pltpu.VMEM((NH, nz, b // nz, bh), f32),
                half, half,
                pltpu.SemaphoreType.DMA((3, na // n_col)),
                pltpu.SemaphoreType.DMA((NH, rt)),
                pltpu.SemaphoreType.DMA((NH, rt)),
                sems, sems, sems, sems, sems, sems,
                pltpu.SemaphoreType.DMA((NH, 4)),
                zsem, zsem, zsem, zsem,
            ],
            compiler_params=pltpu.CompilerParams(collective_id=0, has_side_effects=True, vmem_limit_bytes=56 * 2**20),
            cost_estimate=pl.CostEstimate(flops=4 * 10**9, bytes_accessed=2**23, transcendentals=0),
        )(ancestor_inverse, l_panel, diag_inverse, pattern)

    return jax.shard_map(
        per_device,
        mesh=mesh,
        in_specs=(P(("pole", "prow"), "pcol"), P(("pole", "prow"), "pcol"), P(("pole", "pcol"), None), P()),
        out_specs=(P(("pole", "prow"), "pcol"), P(("pole", "pcol"), None)),
        check_vma=False,
    )
```

```python
import functools

import jax
import jax.numpy as jnp
from jax import lax
from jax.experimental import pallas as pl
from jax.experimental.pallas import tpu as pltpu
from jax.sharding import PartitionSpec as P

MESH = pl.DeviceIdType.MESH
NY = 2
N_COL = 2
NH = 2
SKEW = 3


def kernel(cfg, a_hbm, l_ref, d_ref, pat, out_ref, diag_ref, a_full, own, ubuf, dbuf, sd, su, fin, yin, acc,
           part, yr, ysum, zr, tot, ytot, a_sem, ph_ss, ph_rs, sd_ss, u_rs, su_ss, d_rs, fin_ss, y_rs, r_sem, zs_ss, zs_rs,
           zg_ss, zg_rs):
    nz, rt, share, na, s_n, b = cfg
    bh = b // NH
    tz = rt * NY
    row = lax.axis_index("prow")
    c = lax.axis_index("pcol")
    y = lax.rem(row, NY)
    z = row // NY
    oy = NY - 1 - y
    ypeer = {"prow": z * NY + oy}
    cpeer = {"pcol": 1 - c}

    def zdev(zz):
        return {"prow": zz * NY + y}

    barrier = pltpu.get_barrier_semaphore()
    pl.semaphore_signal(barrier, inc=1, device_id=ypeer, device_id_type=MESH)
    pl.semaphore_signal(barrier, inc=1, device_id=cpeer, device_id_type=MESH)
    for d in range(1, nz):
        pl.semaphore_signal(barrier, inc=1, device_id=zdev(lax.rem(z + d, nz)), device_id_type=MESH)
    acc[...] = jnp.zeros_like(acc)
    n_a = na // N_COL

    def a_local(i):
        return pltpu.make_async_copy(a_hbm.at[:, i * b:(i + 1) * b], a_full.at[c, i], a_sem.at[0, i])

    for i in range(n_a):
        a_local(i).start()
    pl.semaphore_wait(barrier, nz + 1)

    def remote(src, dst, ss, rs, dev):
        return pltpu.make_async_remote_copy(src_ref=src, dst_ref=dst, send_sem=ss, recv_sem=rs, device_id=dev,
                                            device_id_type=MESH)

    def a_send(i):
        return remote(a_hbm.at[:, i * b:(i + 1) * b], a_full.at[c, i], a_sem.at[1, i], a_sem.at[2, i], cpeer)

    def phase1(h, i):
        lanes = pl.ds(pl.multiple_of(oy * b + h * bh, 128), bh)
        return remote(l_ref.at[i * b:(i + 1) * b, lanes], own.at[h, y * rt + i], ph_ss.at[h, i], ph_rs.at[h, i], ypeer)

    for h in range(NH):
        for i in range(rt):
            phase1(h, i).start()
    for i in range(n_a):
        a_send(i).start()
    for h in range(NH):
        lanes = pl.ds(pl.multiple_of(y * b + h * bh, 128), bh)
        for i in range(rt):
            own[h, y * rt + i] = l_ref[i * b:(i + 1) * b, lanes]
    for i in range(rt):
        phase1(0, i).wait_recv()

    below = lax.rem(z + nz - 1, nz)
    above = lax.rem(z + 1, nz)

    def down(h, j):
        return remote(sd.at[h, j], ubuf.at[h, j], sd_ss.at[h, j], u_rs.at[h, j], zdev(below))

    def up(h, j):
        return remote(su.at[h, j], dbuf.at[h, j], su_ss.at[h, j], d_rs.at[h, j], zdev(above))

    def across(h, j):
        return remote(fin.at[h, j], yin.at[h, j], fin_ss.at[h, j], y_rs.at[h, j], ypeer)

    nodes = l_ref.shape[1] // b
    zc = min((na - s_n) // tz, nz - 1)
    j0 = jnp.maximum(tz * z - (na - s_n), 0)
    lag_d = SKEW * jnp.maximum(zc - z, 0)
    lag_u = SKEW * z
    lag_f = jnp.maximum(lag_d, lag_u)
    total = NH * s_n

    def tile_of(k, j):
        return pat[c * nodes + k, j]

    def own_tile(h, t):
        v = own[h, 0]
        for i in range(1, tz):
            v = lax.select(t == tz * z + i, own[h, i], v)
        return v

    def a_tile(t):
        part_at = lax.rem(t, rt) // share
        li = (t // rt) * share + lax.rem(t, share)
        return a_full[part_at, li]

    ch = b // nz
    at_y = pl.ds(pl.multiple_of(y * b, 8), b)
    at_o = pl.ds(pl.multiple_of(oy * b, 8), b)
    mine = pl.ds(pl.multiple_of(z * ch, 8), ch)

    def first(h):
        return remote(part.at[h, oy], yr.at[h], r_sem.at[h, 0], r_sem.at[h, 1], ypeer)

    def last(h):
        return remote(tot.at[h], ytot.at[h], r_sem.at[h, 2], r_sem.at[h, 3], ypeer)

    def rs(h, d):
        to = lax.rem(z + d, nz)
        return remote(ysum.at[h, pl.ds(pl.multiple_of(to * ch, 8), ch), :], zr.at[h, d], zs_ss.at[h, d],
                      zs_rs.at[h, d], zdev(to))

    def ag(h, d):
        to = lax.rem(z + d, nz)
        return remote(tot.at[h, mine, :], tot.at[h, mine, :], zg_ss.at[h, d], zg_rs.at[h, d], zdev(to))

    def ag_in(h, d):
        at = lax.rem(z + nz - d, nz)
        there = pl.ds(pl.multiple_of(at * ch, 8), ch)
        return remote(tot.at[h, there, :], tot.at[h, there, :], zg_ss.at[h, d], zg_rs.at[h, d], zdev(at))

    def reduce_0(h):
        for k in range(nodes):
            at = slice(k * b + h * bh, k * b + (h + 1) * bh)
            for i in range(rt):
                t = row * rt + i
                hit = pat[c * nodes + k, 0] == t
                for j in range(1, s_n):
                    hit = hit | (pat[c * nodes + k, j] == t)
                m = -jnp.where(hit, 1.0, 0.0).astype(jnp.float32)
                out_ref[i * b:(i + 1) * b, at] = acc[k, h, i * b:(i + 1) * b, :] * m
            x = out_ref[:, at]
            hi = x.astype(jnp.bfloat16)
            lo = (x - hi.astype(jnp.float32)).astype(jnp.bfloat16)
            both = lax.dot_general(l_ref[:, k * b:(k + 1) * b], jnp.concatenate([hi, lo], axis=1),
                                   (((0,), (0,)), ((), ())), preferred_element_type=jnp.float32)
            part[h, k] = both[:, :bh] + both[:, bh:]
        first(h).start()

    def reduce_1(h):
        first(h).wait()
        ysum[h] = part[h, y] + yr[h]
        for d in range(1, nz):
            rs(h, d).start()

    def reduce_2(h):
        total_z = ysum[h, mine, :]
        for d in range(1, nz):
            rs(h, d).wait_recv()
            total_z = total_z + zr[h, d]
        tot[h, mine, :] = total_z
        for d in range(1, nz):
            ag(h, d).start()

    def reduce_3(h):
        for d in range(1, nz):
            ag_in(h, d).wait_recv()
        last(h).start()
        lanes = slice(h * bh, (h + 1) * bh)
        diag_ref[at_y, lanes] = d_ref[at_y, lanes] - tot[h]

    def reduce_4(h):
        lanes = slice(h * bh, (h + 1) * bh)
        last(h).wait_recv()
        diag_ref[at_o, lanes] = d_ref[at_o, lanes] - ytot[h]

    def step(s, carry):
        @pl.when(s == s_n)
        def _():
            for h in range(1, NH):
                for i in range(rt):
                    phase1(h, i).wait_recv()

        @pl.when(s == lag_f)
        def _():
            for i in range(n_a):
                a_local(i).wait()
                a_send(i).wait()

        pd = s - lag_d
        hd, jd = pd // s_n, j0 + lax.rem(pd, s_n)
        live = (pd >= 0) & (pd < total) & (jd < s_n)

        @pl.when(live & (z < nz - 1) & (jd + (na - s_n) >= tz * (z + 1)))
        def _():
            down(hd, jd).wait_recv()

        @pl.when(live & (z > 0))
        def _():
            t = tile_of(y, jd)
            sd[hd, jd] = lax.select(t < tz * (z + 1), own_tile(hd, t), ubuf[hd, jd])
            down(hd, jd).start()

        pu = s - lag_u
        hu, ju = pu // s_n, lax.rem(pu, s_n)
        live_u = (pu >= 0) & (pu < total) & (ju < s_n - 1)

        @pl.when(live_u & (z > 0) & (ju < tz * z))
        def _():
            up(hu, ju).wait_recv()

        @pl.when(live_u & (z < nz - 1) & (ju < tz * (z + 1)))
        def _():
            t = tile_of(y, ju)
            su[hu, ju] = lax.select(t >= tz * z, own_tile(hu, t), dbuf[hu, ju])
            up(hu, ju).start()

        pf = s - lag_f
        hf, jf = pf // s_n, lax.rem(pf, s_n)

        @pl.when((pf >= 0) & (pf < total))
        def _():
            t = tile_of(y, jf)
            v = lax.select(t < tz * z, dbuf[hf, jf], own_tile(hf, t))
            v = lax.select(t >= tz * (z + 1), ubuf[hf, jf], v)
            fin[hf, jf] = v
            across(hf, jf).start()
            acc[y, hf] += jnp.dot(a_tile(t), v, preferred_element_type=jnp.float32)

        py = pf - SKEW
        hy, jy = py // s_n, lax.rem(py, s_n)

        @pl.when((py >= 0) & (py < total))
        def _():
            across(hy, jy).wait_recv()
            t = tile_of(oy, jy)
            acc[oy, hy] += jnp.dot(a_tile(t), yin[hy, jy], preferred_element_type=jnp.float32)

        for h in range(NH - 1):
            done = (h + 1) * s_n + SKEW

            @pl.when(s == done + lag_f)
            def _(h=h):
                reduce_0(h)

        return carry

    lax.fori_loop(0, total + SKEW * nz, step, 0)

    h = NH - 1
    for g in range(h):
        reduce_1(g)
    reduce_0(h)
    for phase, following in ((reduce_1, reduce_2), (reduce_2, reduce_3), (reduce_3, reduce_4)):
        for g in range(h):
            following(g)
        phase(h)

    for g in range(NH):
        for i in range(rt):
            phase1(g, i).wait_send()

    def drain(p, carry):
        g, j = p // s_n, lax.rem(p, s_n)

        @pl.when((z > 0) & (j >= j0))
        def _():
            down(g, j).wait_send()

        @pl.when((z < nz - 1) & (j < s_n - 1) & (j < tz * (z + 1)))
        def _():
            up(g, j).wait_send()

        across(g, j).wait_send()
        return carry

    lax.fori_loop(0, total, drain, 0)
    for g in range(NH):
        for d in range(1, nz):
            rs(g, d).wait_send()
            ag(g, d).wait_send()
        last(g).wait_send()
    reduce_4(h)


def solution(mesh):
    n_row, n_col = mesh.shape["prow"], mesh.shape["pcol"]
    nz = n_row // NY

    def per_device(ancestor_inverse, l_panel, diag_inverse, pattern):
        b = diag_inverse.shape[1]
        rt = l_panel.shape[0] // b
        nodes = l_panel.shape[1] // b
        na, s_n = rt * n_row, pattern.shape[1]
        share = rt // n_col
        bh = b // NH
        bf, f32 = jnp.bfloat16, jnp.float32
        slots = pltpu.VMEM((NH, s_n, b, bh), bf)
        sems = pltpu.SemaphoreType.DMA((NH, s_n))
        zsem = pltpu.SemaphoreType.DMA((NH, nz))
        half = pltpu.VMEM((NH, b, bh), f32)
        vmem = pl.BlockSpec(memory_space=pltpu.VMEM)
        return pl.pallas_call(
            functools.partial(kernel, (nz, rt, share, na, s_n, b)),
            out_shape=(jax.ShapeDtypeStruct(l_panel.shape, f32), jax.ShapeDtypeStruct(diag_inverse.shape, f32)),
            in_specs=[pl.BlockSpec(memory_space=pl.ANY), vmem, vmem, pl.BlockSpec(memory_space=pltpu.SMEM)],
            out_specs=(vmem, vmem),
            scratch_shapes=[
                pltpu.VMEM((n_col, na // n_col, rt * b, b), bf),
                pltpu.VMEM((NH, rt * NY, b, bh), bf),
                slots, slots, slots, slots, slots, slots,
                pltpu.VMEM((nodes, NH, rt * b, bh), f32),
                pltpu.VMEM((NH, nodes, b, bh), f32),
                half, half,
                pltpu.VMEM((NH, nz, b // nz, bh), f32),
                half, half,
                pltpu.SemaphoreType.DMA((3, na // n_col)),
                pltpu.SemaphoreType.DMA((NH, rt)),
                pltpu.SemaphoreType.DMA((NH, rt)),
                sems, sems, sems, sems, sems, sems,
                pltpu.SemaphoreType.DMA((NH, 4)),
                zsem, zsem, zsem, zsem,
            ],
            compiler_params=pltpu.CompilerParams(collective_id=0, has_side_effects=True, vmem_limit_bytes=56 * 2**20),
            cost_estimate=pl.CostEstimate(flops=4 * 10**9, bytes_accessed=2**23, transcendentals=0),
        )(ancestor_inverse, l_panel, diag_inverse, pattern)

    return jax.shard_map(
        per_device,
        mesh=mesh,
        in_specs=(P(("pole", "prow"), "pcol"), P(("pole", "prow"), "pcol"), P(("pole", "pcol"), None), P()),
        out_specs=(P(("pole", "prow"), "pcol"), P(("pole", "pcol"), None)),
        check_vma=False,
    )
```

```python
import functools

import jax
import jax.numpy as jnp
from jax import lax
from jax.experimental import pallas as pl
from jax.experimental.pallas import tpu as pltpu
from jax.sharding import PartitionSpec as P

MESH = pl.DeviceIdType.MESH
NY = 2
N_COL = 2
NH = 2
GAP = 5
SKEW = 4


def kernel(cfg, a_hbm, l_ref, d_ref, pat, out_ref, diag_ref, a_full, own, ubuf, dbuf, sd, su, fin, yin, acc,
           part, yr, ysum, zr, tot, ytot, a_sem, ph_ss, ph_rs, sd_ss, u_rs, su_ss, d_rs, fin_ss, y_rs, r_sem, zs_ss, zs_rs,
           zg_ss, zg_rs):
    nz, rt, share, na, s_n, b = cfg
    bh = b // NH
    tz = rt * NY
    row = lax.axis_index("prow")
    c = lax.axis_index("pcol")
    y = lax.rem(row, NY)
    z = row // NY
    oy = NY - 1 - y
    ypeer = {"prow": z * NY + oy}
    cpeer = {"pcol": 1 - c}

    def zdev(zz):
        return {"prow": zz * NY + y}

    barrier = pltpu.get_barrier_semaphore()
    pl.semaphore_signal(barrier, inc=1, device_id=ypeer, device_id_type=MESH)
    pl.semaphore_signal(barrier, inc=1, device_id=cpeer, device_id_type=MESH)
    for d in range(1, nz):
        pl.semaphore_signal(barrier, inc=1, device_id=zdev(lax.rem(z + d, nz)), device_id_type=MESH)
    acc[...] = jnp.zeros_like(acc)
    n_a = na // N_COL

    def a_local(i):
        return pltpu.make_async_copy(a_hbm.at[:, i * b:(i + 1) * b], a_full.at[c, i], a_sem.at[0, i])

    for i in range(n_a):
        a_local(i).start()
    pl.semaphore_wait(barrier, nz + 1)

    def remote(src, dst, ss, rs, dev):
        return pltpu.make_async_remote_copy(src_ref=src, dst_ref=dst, send_sem=ss, recv_sem=rs, device_id=dev,
                                            device_id_type=MESH)

    def a_send(i):
        return remote(a_hbm.at[:, i * b:(i + 1) * b], a_full.at[c, i], a_sem.at[1, i], a_sem.at[2, i], cpeer)

    def phase1(h, i):
        lanes = pl.ds(pl.multiple_of(oy * b + h * bh, 128), bh)
        return remote(l_ref.at[i * b:(i + 1) * b, lanes], own.at[h, y * rt + i], ph_ss.at[h, i], ph_rs.at[h, i], ypeer)

    for h in range(NH):
        for i in range(rt):
            phase1(h, i).start()
    for i in range(n_a):
        a_send(i).start()
    for h in range(NH):
        lanes = pl.ds(pl.multiple_of(y * b + h * bh, 128), bh)
        for i in range(rt):
            own[h, y * rt + i] = l_ref[i * b:(i + 1) * b, lanes]
    for i in range(rt):
        phase1(0, i).wait_recv()

    below = lax.rem(z + nz - 1, nz)
    above = lax.rem(z + 1, nz)

    def down(h, j):
        return remote(sd.at[h, j], ubuf.at[h, j], sd_ss.at[h, j], u_rs.at[h, j], zdev(below))

    def up(h, j):
        return remote(su.at[h, j], dbuf.at[h, j], su_ss.at[h, j], d_rs.at[h, j], zdev(above))

    def across(h, j):
        return remote(fin.at[h, j], yin.at[h, j], fin_ss.at[h, j], y_rs.at[h, j], ypeer)

    nodes = l_ref.shape[1] // b
    zc = min((na - s_n) // tz, nz - 1)
    j0 = jnp.maximum(tz * z - (na - s_n), 0)
    lag_d = SKEW * jnp.maximum(zc - z, 0)
    lag_u = SKEW * z
    lag_f = jnp.maximum(lag_d, lag_u)
    total = NH * s_n

    def tile_of(k, j):
        return pat[c * nodes + k, j]

    def own_tile(h, t):
        v = own[h, 0]
        for i in range(1, tz):
            v = lax.select(t == tz * z + i, own[h, i], v)
        return v

    def a_tile(t):
        part_at = lax.rem(t, rt) // share
        li = (t // rt) * share + lax.rem(t, share)
        return a_full[part_at, li]

    ch = b // nz
    at_y = pl.ds(pl.multiple_of(y * b, 8), b)
    at_o = pl.ds(pl.multiple_of(oy * b, 8), b)
    mine = pl.ds(pl.multiple_of(z * ch, 8), ch)

    def first(h):
        return remote(part.at[h, oy], yr.at[h], r_sem.at[h, 0], r_sem.at[h, 1], ypeer)

    def last(h):
        return remote(tot.at[h], ytot.at[h], r_sem.at[h, 2], r_sem.at[h, 3], ypeer)

    def rs(h, d):
        to = lax.rem(z + d, nz)
        return remote(ysum.at[h, pl.ds(pl.multiple_of(to * ch, 8), ch), :], zr.at[h, d], zs_ss.at[h, d],
                      zs_rs.at[h, d], zdev(to))

    def ag(h, d):
        to = lax.rem(z + d, nz)
        return remote(tot.at[h, mine, :], tot.at[h, mine, :], zg_ss.at[h, d], zg_rs.at[h, d], zdev(to))

    def ag_in(h, d):
        at = lax.rem(z + nz - d, nz)
        there = pl.ds(pl.multiple_of(at * ch, 8), ch)
        return remote(tot.at[h, there, :], tot.at[h, there, :], zg_ss.at[h, d], zg_rs.at[h, d], zdev(at))

    def reduce_0(h):
        for k in range(nodes):
            at = slice(k * b + h * bh, k * b + (h + 1) * bh)
            for i in range(rt):
                t = row * rt + i
                hit = pat[c * nodes + k, 0] == t
                for j in range(1, s_n):
                    hit = hit | (pat[c * nodes + k, j] == t)
                m = -jnp.where(hit, 1.0, 0.0).astype(jnp.float32)
                out_ref[i * b:(i + 1) * b, at] = acc[k, h, i * b:(i + 1) * b, :] * m
            x = out_ref[:, at]
            hi = x.astype(jnp.bfloat16)
            lo = (x - hi.astype(jnp.float32)).astype(jnp.bfloat16)
            both = lax.dot_general(l_ref[:, k * b:(k + 1) * b], jnp.concatenate([hi, lo], axis=1),
                                   (((0,), (0,)), ((), ())), preferred_element_type=jnp.float32)
            part[h, k] = both[:, :bh] + both[:, bh:]
        first(h).start()

    def reduce_1(h):
        first(h).wait()
        ysum[h] = part[h, y] + yr[h]
        for d in range(1, nz):
            rs(h, d).start()

    def reduce_2(h):
        total_z = ysum[h, mine, :]
        for d in range(1, nz):
            rs(h, d).wait_recv()
            total_z = total_z + zr[h, d]
        tot[h, mine, :] = total_z
        for d in range(1, nz):
            ag(h, d).start()

    def reduce_3(h):
        for d in range(1, nz):
            ag_in(h, d).wait_recv()
        last(h).start()
        lanes = slice(h * bh, (h + 1) * bh)
        diag_ref[at_y, lanes] = d_ref[at_y, lanes] - tot[h]

    def reduce_4(h):
        lanes = slice(h * bh, (h + 1) * bh)
        last(h).wait_recv()
        diag_ref[at_o, lanes] = d_ref[at_o, lanes] - ytot[h]

    def step(s, carry):
        @pl.when(s == s_n)
        def _():
            for h in range(1, NH):
                for i in range(rt):
                    phase1(h, i).wait_recv()

        @pl.when(s == lag_f)
        def _():
            for i in range(n_a):
                a_local(i).wait()
                a_send(i).wait()

        pd = s - lag_d
        hd, jd = pd // s_n, j0 + lax.rem(pd, s_n)
        live = (pd >= 0) & (pd < total) & (jd < s_n)

        @pl.when(live & (z < nz - 1) & (jd + (na - s_n) >= tz * (z + 1)))
        def _():
            down(hd, jd).wait_recv()

        @pl.when(live & (z > 0))
        def _():
            t = tile_of(y, jd)
            sd[hd, jd] = lax.select(t < tz * (z + 1), own_tile(hd, t), ubuf[hd, jd])
            down(hd, jd).start()

        pu = s - lag_u
        hu, ju = pu // s_n, lax.rem(pu, s_n)
        live_u = (pu >= 0) & (pu < total) & (ju < s_n - 1)

        @pl.when(live_u & (z > 0) & (ju < tz * z))
        def _():
            up(hu, ju).wait_recv()

        @pl.when(live_u & (z < nz - 1) & (ju < tz * (z + 1)))
        def _():
            t = tile_of(y, ju)
            su[hu, ju] = lax.select(t >= tz * z, own_tile(hu, t), dbuf[hu, ju])
            up(hu, ju).start()

        pf = s - lag_f
        hf, jf = pf // s_n, lax.rem(pf, s_n)

        @pl.when((pf >= 0) & (pf < total))
        def _():
            t = tile_of(y, jf)
            v = lax.select(t < tz * z, dbuf[hf, jf], own_tile(hf, t))
            v = lax.select(t >= tz * (z + 1), ubuf[hf, jf], v)
            fin[hf, jf] = v
            across(hf, jf).start()
            acc[y, hf] += jnp.dot(a_tile(t), v, preferred_element_type=jnp.float32)

        py = pf - SKEW
        hy, jy = py // s_n, lax.rem(py, s_n)

        @pl.when((py >= 0) & (py < total))
        def _():
            across(hy, jy).wait_recv()
            t = tile_of(oy, jy)
            acc[oy, hy] += jnp.dot(a_tile(t), yin[hy, jy], preferred_element_type=jnp.float32)

        for h in range(NH - 1):
            done = (h + 1) * s_n + SKEW

            @pl.when(s == done + lag_f)
            def _(h=h):
                reduce_0(h)

            @pl.when(s == done + lag_f + min(GAP, s_n - 1))
            def _(h=h):
                reduce_1(h)

        return carry

    lax.fori_loop(0, total + SKEW * nz, step, 0)

    h = NH - 1
    reduce_0(h)
    for phase, following in ((reduce_1, reduce_2), (reduce_2, reduce_3), (reduce_3, reduce_4)):
        for g in range(h):
            following(g)
        phase(h)

    for g in range(NH):
        for i in range(rt):
            phase1(g, i).wait_send()

    def drain(p, carry):
        g, j = p // s_n, lax.rem(p, s_n)

        @pl.when((z > 0) & (j >= j0))
        def _():
            down(g, j).wait_send()

        @pl.when((z < nz - 1) & (j < s_n - 1) & (j < tz * (z + 1)))
        def _():
            up(g, j).wait_send()

        across(g, j).wait_send()
        return carry

    lax.fori_loop(0, total, drain, 0)
    for g in range(NH):
        for d in range(1, nz):
            rs(g, d).wait_send()
            ag(g, d).wait_send()
        last(g).wait_send()
    reduce_4(h)


def solution(mesh):
    n_row, n_col = mesh.shape["prow"], mesh.shape["pcol"]
    nz = n_row // NY

    def per_device(ancestor_inverse, l_panel, diag_inverse, pattern):
        b = diag_inverse.shape[1]
        rt = l_panel.shape[0] // b
        nodes = l_panel.shape[1] // b
        na, s_n = rt * n_row, pattern.shape[1]
        share = rt // n_col
        bh = b // NH
        bf, f32 = jnp.bfloat16, jnp.float32
        slots = pltpu.VMEM((NH, s_n, b, bh), bf)
        sems = pltpu.SemaphoreType.DMA((NH, s_n))
        zsem = pltpu.SemaphoreType.DMA((NH, nz))
        half = pltpu.VMEM((NH, b, bh), f32)
        vmem = pl.BlockSpec(memory_space=pltpu.VMEM)
        return pl.pallas_call(
            functools.partial(kernel, (nz, rt, share, na, s_n, b)),
            out_shape=(jax.ShapeDtypeStruct(l_panel.shape, f32), jax.ShapeDtypeStruct(diag_inverse.shape, f32)),
            in_specs=[pl.BlockSpec(memory_space=pl.ANY), vmem, vmem, pl.BlockSpec(memory_space=pltpu.SMEM)],
            out_specs=(vmem, vmem),
            scratch_shapes=[
                pltpu.VMEM((n_col, na // n_col, rt * b, b), bf),
                pltpu.VMEM((NH, rt * NY, b, bh), bf),
                slots, slots, slots, slots, slots, slots,
                pltpu.VMEM((nodes, NH, rt * b, bh), f32),
                pltpu.VMEM((NH, nodes, b, bh), f32),
                half, half,
                pltpu.VMEM((NH, nz, b // nz, bh), f32),
                half, half,
                pltpu.SemaphoreType.DMA((3, na // n_col)),
                pltpu.SemaphoreType.DMA((NH, rt)),
                pltpu.SemaphoreType.DMA((NH, rt)),
                sems, sems, sems, sems, sems, sems,
                pltpu.SemaphoreType.DMA((NH, 4)),
                zsem, zsem, zsem, zsem,
            ],
            compiler_params=pltpu.CompilerParams(collective_id=0, has_side_effects=True, vmem_limit_bytes=56 * 2**20),
            cost_estimate=pl.CostEstimate(flops=4 * 10**9, bytes_accessed=2**23, transcendentals=0),
        )(ancestor_inverse, l_panel, diag_inverse, pattern)

    return jax.shard_map(
        per_device,
        mesh=mesh,
        in_specs=(P(("pole", "prow"), "pcol"), P(("pole", "prow"), "pcol"), P(("pole", "pcol"), None), P()),
        out_specs=(P(("pole", "prow"), "pcol"), P(("pole", "pcol"), None)),
        check_vma=False,
    )
```

```python
import functools

import jax
import jax.numpy as jnp
from jax import lax
from jax.experimental import pallas as pl
from jax.experimental.pallas import tpu as pltpu
from jax.sharding import PartitionSpec as P

MESH = pl.DeviceIdType.MESH
NY = 2
N_COL = 2
NH = 2
GAP = 7
SKEW = 6


def kernel(cfg, a_hbm, l_ref, d_ref, pat, out_ref, diag_ref, a_full, own, ubuf, dbuf, sd, su, fin, yin, acc,
           part, yr, ysum, zr, tot, ytot, a_sem, ph_ss, ph_rs, sd_ss, u_rs, su_ss, d_rs, fin_ss, y_rs, r_sem, zs_ss, zs_rs,
           zg_ss, zg_rs):
    nz, rt, share, na, s_n, b = cfg
    bh = b // NH
    tz = rt * NY
    row = lax.axis_index("prow")
    c = lax.axis_index("pcol")
    y = lax.rem(row, NY)
    z = row // NY
    oy = NY - 1 - y
    ypeer = {"prow": z * NY + oy}
    cpeer = {"pcol": 1 - c}

    def zdev(zz):
        return {"prow": zz * NY + y}

    barrier = pltpu.get_barrier_semaphore()
    pl.semaphore_signal(barrier, inc=1, device_id=ypeer, device_id_type=MESH)
    pl.semaphore_signal(barrier, inc=1, device_id=cpeer, device_id_type=MESH)
    for d in range(1, nz):
        pl.semaphore_signal(barrier, inc=1, device_id=zdev(lax.rem(z + d, nz)), device_id_type=MESH)
    acc[...] = jnp.zeros_like(acc)
    n_a = na // N_COL

    def a_local(i):
        return pltpu.make_async_copy(a_hbm.at[:, i * b:(i + 1) * b], a_full.at[c, i], a_sem.at[0, i])

    for i in range(n_a):
        a_local(i).start()
    pl.semaphore_wait(barrier, nz + 1)

    def remote(src, dst, ss, rs, dev):
        return pltpu.make_async_remote_copy(src_ref=src, dst_ref=dst, send_sem=ss, recv_sem=rs, device_id=dev,
                                            device_id_type=MESH)

    def a_send(i):
        return remote(a_hbm.at[:, i * b:(i + 1) * b], a_full.at[c, i], a_sem.at[1, i], a_sem.at[2, i], cpeer)

    def phase1(h, i):
        lanes = pl.ds(pl.multiple_of(oy * b + h * bh, 128), bh)
        return remote(l_ref.at[i * b:(i + 1) * b, lanes], own.at[h, y * rt + i], ph_ss.at[h, i], ph_rs.at[h, i], ypeer)

    for h in range(NH):
        for i in range(rt):
            phase1(h, i).start()
    for i in range(n_a):
        a_send(i).start()
    for h in range(NH):
        lanes = pl.ds(pl.multiple_of(y * b + h * bh, 128), bh)
        for i in range(rt):
            own[h, y * rt + i] = l_ref[i * b:(i + 1) * b, lanes]
    for i in range(rt):
        phase1(0, i).wait_recv()

    below = lax.rem(z + nz - 1, nz)
    above = lax.rem(z + 1, nz)

    def down(h, j):
        return remote(sd.at[h, j], ubuf.at[h, j], sd_ss.at[h, j], u_rs.at[h, j], zdev(below))

    def up(h, j):
        return remote(su.at[h, j], dbuf.at[h, j], su_ss.at[h, j], d_rs.at[h, j], zdev(above))

    def across(h, j):
        return remote(fin.at[h, j], yin.at[h, j], fin_ss.at[h, j], y_rs.at[h, j], ypeer)

    nodes = l_ref.shape[1] // b
    zc = min((na - s_n) // tz, nz - 1)
    j0 = jnp.maximum(tz * z - (na - s_n), 0)
    lag_d = SKEW * jnp.maximum(zc - z, 0)
    lag_u = SKEW * z
    lag_f = jnp.maximum(lag_d, lag_u)
    total = NH * s_n

    def tile_of(k, j):
        return pat[c * nodes + k, j]

    def own_tile(h, t):
        v = own[h, 0]
        for i in range(1, tz):
            v = lax.select(t == tz * z + i, own[h, i], v)
        return v

    def a_tile(t):
        part_at = lax.rem(t, rt) // share
        li = (t // rt) * share + lax.rem(t, share)
        return a_full[part_at, li]

    ch = b // nz
    at_y = pl.ds(pl.multiple_of(y * b, 8), b)
    at_o = pl.ds(pl.multiple_of(oy * b, 8), b)
    mine = pl.ds(pl.multiple_of(z * ch, 8), ch)

    def first(h):
        return remote(part.at[h, oy], yr.at[h], r_sem.at[h, 0], r_sem.at[h, 1], ypeer)

    def last(h):
        return remote(tot.at[h], ytot.at[h], r_sem.at[h, 2], r_sem.at[h, 3], ypeer)

    def rs(h, d):
        to = lax.rem(z + d, nz)
        return remote(ysum.at[h, pl.ds(pl.multiple_of(to * ch, 8), ch), :], zr.at[h, d], zs_ss.at[h, d],
                      zs_rs.at[h, d], zdev(to))

    def ag(h, d):
        to = lax.rem(z + d, nz)
        return remote(tot.at[h, mine, :], tot.at[h, mine, :], zg_ss.at[h, d], zg_rs.at[h, d], zdev(to))

    def ag_in(h, d):
        at = lax.rem(z + nz - d, nz)
        there = pl.ds(pl.multiple_of(at * ch, 8), ch)
        return remote(tot.at[h, there, :], tot.at[h, there, :], zg_ss.at[h, d], zg_rs.at[h, d], zdev(at))

    def reduce_0(h):
        for k in range(nodes):
            at = slice(k * b + h * bh, k * b + (h + 1) * bh)
            for i in range(rt):
                t = row * rt + i
                hit = pat[c * nodes + k, 0] == t
                for j in range(1, s_n):
                    hit = hit | (pat[c * nodes + k, j] == t)
                m = -jnp.where(hit, 1.0, 0.0).astype(jnp.float32)
                out_ref[i * b:(i + 1) * b, at] = acc[k, h, i * b:(i + 1) * b, :] * m
            x = out_ref[:, at]
            hi = x.astype(jnp.bfloat16)
            lo = (x - hi.astype(jnp.float32)).astype(jnp.bfloat16)
            both = lax.dot_general(l_ref[:, k * b:(k + 1) * b], jnp.concatenate([hi, lo], axis=1),
                                   (((0,), (0,)), ((), ())), preferred_element_type=jnp.float32)
            part[h, k] = both[:, :bh] + both[:, bh:]
        first(h).start()

    def reduce_1(h):
        first(h).wait()
        ysum[h] = part[h, y] + yr[h]
        for d in range(1, nz):
            rs(h, d).start()

    def reduce_2(h):
        total_z = ysum[h, mine, :]
        for d in range(1, nz):
            rs(h, d).wait_recv()
            total_z = total_z + zr[h, d]
        tot[h, mine, :] = total_z
        for d in range(1, nz):
            ag(h, d).start()

    def reduce_3(h):
        for d in range(1, nz):
            ag_in(h, d).wait_recv()
        last(h).start()
        lanes = slice(h * bh, (h + 1) * bh)
        diag_ref[at_y, lanes] = d_ref[at_y, lanes] - tot[h]

    def reduce_4(h):
        lanes = slice(h * bh, (h + 1) * bh)
        last(h).wait_recv()
        diag_ref[at_o, lanes] = d_ref[at_o, lanes] - ytot[h]

    def step(s, carry):
        @pl.when(s == s_n)
        def _():
            for h in range(1, NH):
                for i in range(rt):
                    phase1(h, i).wait_recv()

        @pl.when(s == lag_f)
        def _():
            for i in range(n_a):
                a_local(i).wait()
                a_send(i).wait()

        pd = s - lag_d
        hd, jd = pd // s_n, j0 + lax.rem(pd, s_n)
        live = (pd >= 0) & (pd < total) & (jd < s_n)

        @pl.when(live & (z < nz - 1) & (jd + (na - s_n) >= tz * (z + 1)))
        def _():
            down(hd, jd).wait_recv()

        @pl.when(live & (z > 0))
        def _():
            t = tile_of(y, jd)
            sd[hd, jd] = lax.select(t < tz * (z + 1), own_tile(hd, t), ubuf[hd, jd])
            down(hd, jd).start()

        pu = s - lag_u
        hu, ju = pu // s_n, lax.rem(pu, s_n)
        live_u = (pu >= 0) & (pu < total) & (ju < s_n - 1)

        @pl.when(live_u & (z > 0) & (ju < tz * z))
        def _():
            up(hu, ju).wait_recv()

        @pl.when(live_u & (z < nz - 1) & (ju < tz * (z + 1)))
        def _():
            t = tile_of(y, ju)
            su[hu, ju] = lax.select(t >= tz * z, own_tile(hu, t), dbuf[hu, ju])
            up(hu, ju).start()

        pf = s - lag_f
        hf, jf = pf // s_n, lax.rem(pf, s_n)

        @pl.when((pf >= 0) & (pf < total))
        def _():
            t = tile_of(y, jf)
            v = lax.select(t < tz * z, dbuf[hf, jf], own_tile(hf, t))
            v = lax.select(t >= tz * (z + 1), ubuf[hf, jf], v)
            fin[hf, jf] = v
            across(hf, jf).start()
            acc[y, hf] += jnp.dot(a_tile(t), v, preferred_element_type=jnp.float32)

        py = pf - SKEW
        hy, jy = py // s_n, lax.rem(py, s_n)

        @pl.when((py >= 0) & (py < total))
        def _():
            across(hy, jy).wait_recv()
            t = tile_of(oy, jy)
            acc[oy, hy] += jnp.dot(a_tile(t), yin[hy, jy], preferred_element_type=jnp.float32)

        for h in range(NH - 1):
            done = (h + 1) * s_n + SKEW

            @pl.when(s == done + lag_f)
            def _(h=h):
                reduce_0(h)

            @pl.when(s == done + lag_f + min(GAP, s_n - 1))
            def _(h=h):
                reduce_1(h)

        return carry

    lax.fori_loop(0, total + SKEW * nz, step, 0)

    h = NH - 1
    reduce_0(h)
    for phase, following in ((reduce_1, reduce_2), (reduce_2, reduce_3), (reduce_3, reduce_4)):
        for g in range(h):
            following(g)
        phase(h)

    for g in range(NH):
        for i in range(rt):
            phase1(g, i).wait_send()

    def drain(p, carry):
        g, j = p // s_n, lax.rem(p, s_n)

        @pl.when((z > 0) & (j >= j0))
        def _():
            down(g, j).wait_send()

        @pl.when((z < nz - 1) & (j < s_n - 1) & (j < tz * (z + 1)))
        def _():
            up(g, j).wait_send()

        across(g, j).wait_send()
        return carry

    lax.fori_loop(0, total, drain, 0)
    for g in range(NH):
        for d in range(1, nz):
            rs(g, d).wait_send()
            ag(g, d).wait_send()
        last(g).wait_send()
    reduce_4(h)


def solution(mesh):
    n_row, n_col = mesh.shape["prow"], mesh.shape["pcol"]
    nz = n_row // NY

    def per_device(ancestor_inverse, l_panel, diag_inverse, pattern):
        b = diag_inverse.shape[1]
        rt = l_panel.shape[0] // b
        nodes = l_panel.shape[1] // b
        na, s_n = rt * n_row, pattern.shape[1]
        share = rt // n_col
        bh = b // NH
        bf, f32 = jnp.bfloat16, jnp.float32
        slots = pltpu.VMEM((NH, s_n, b, bh), bf)
        sems = pltpu.SemaphoreType.DMA((NH, s_n))
        zsem = pltpu.SemaphoreType.DMA((NH, nz))
        half = pltpu.VMEM((NH, b, bh), f32)
        vmem = pl.BlockSpec(memory_space=pltpu.VMEM)
        return pl.pallas_call(
            functools.partial(kernel, (nz, rt, share, na, s_n, b)),
            out_shape=(jax.ShapeDtypeStruct(l_panel.shape, f32), jax.ShapeDtypeStruct(diag_inverse.shape, f32)),
            in_specs=[pl.BlockSpec(memory_space=pl.ANY), vmem, vmem, pl.BlockSpec(memory_space=pltpu.SMEM)],
            out_specs=(vmem, vmem),
            scratch_shapes=[
                pltpu.VMEM((n_col, na // n_col, rt * b, b), bf),
                pltpu.VMEM((NH, rt * NY, b, bh), bf),
                slots, slots, slots, slots, slots, slots,
                pltpu.VMEM((nodes, NH, rt * b, bh), f32),
                pltpu.VMEM((NH, nodes, b, bh), f32),
                half, half,
                pltpu.VMEM((NH, nz, b // nz, bh), f32),
                half, half,
                pltpu.SemaphoreType.DMA((3, na // n_col)),
                pltpu.SemaphoreType.DMA((NH, rt)),
                pltpu.SemaphoreType.DMA((NH, rt)),
                sems, sems, sems, sems, sems, sems,
                pltpu.SemaphoreType.DMA((NH, 4)),
                zsem, zsem, zsem, zsem,
            ],
            compiler_params=pltpu.CompilerParams(collective_id=0, has_side_effects=True, vmem_limit_bytes=56 * 2**20),
            cost_estimate=pl.CostEstimate(flops=4 * 10**9, bytes_accessed=2**23, transcendentals=0),
        )(ancestor_inverse, l_panel, diag_inverse, pattern)

    return jax.shard_map(
        per_device,
        mesh=mesh,
        in_specs=(P(("pole", "prow"), "pcol"), P(("pole", "prow"), "pcol"), P(("pole", "pcol"), None), P()),
        out_specs=(P(("pole", "prow"), "pcol"), P(("pole", "pcol"), None)),
        check_vma=False,
    )
```
